512 devices in a mesh: seq: 128 (over z_lo, y, x, core), head: 4 (over z_hi).
Axes of the slice: x: 4, y: 8, z: 8 (z_hi: 4, z_lo: 2; z = z_hi * 2 + z_lo), core: 2. Of those that a mesh axis runs over, the one named last changes fastest.
Arguments:
- queries: bfloat16 [16384, 1536], P('seq', 'head'), may hold values from -240 to 240
- key_states: bfloat16 [16384, 1536], P('seq', 'head'), may hold values from -8 to 8
- value_states: bfloat16 [16384, 1536], P('seq', 'head'), may hold values from -6 to 6
- attn_output: bfloat16 [16384, 1536], P('seq', 'head'), may hold values from -6 to 6
- grad_output: bfloat16 [16384, 1536], P('seq', 'head'), may hold values from -6 to 6
- block_index: int32 [128, 4], P('seq'), may hold values from 0 to 31, as said below
- valid_count: int32 [128], P('seq'), may hold values from 1 to 4, 256 in all
Outputs:
- grad_queries: bfloat16 [16384, 1536], P(('seq', 'head'))
- grad_keys: bfloat16 [16384, 1536], P(('seq', 'head'))
- grad_values: bfloat16 [16384, 1536], P(('seq', 'head'))
The draws below stay inside these ranges and needn't reach their ends.
Inputs may be any that keep to these rules, and one draw needn't show every extreme that they name: `block_index`: each owner's 4 entries are distinct block numbers of its own 128 tokens in blocks of 4; entries at slots from valid_count on are padding. `valid_count`: the counts sum to 256.
All inputs are finite; a program needn't handle non-finite values. No bound on the sum of `valid_count` on one device may be relied on, other than what follows from the above.
Results may differ from the reference program's by a relative error of at most 0.017.
Values may be sent and summed in bfloat16 or wider, within the bound.
A program may use at most 64 MiB of HBM per device.

```python
import math
import jax
import jax.numpy as jnp
import numpy as np
from jax import lax

HEADS = 12
HD = 128
TOK_DEV = 128
BLK = 4
MB_DEV = 4
TOKENS = 16384
VALID_BLOCKS = 256
N_SEQ = 128


def shared_keys(key):
    base = jnp.clip(jax.random.normal(key, (TOKENS, HEADS * HD), jnp.float32), -6.0, 6.0)
    ramp = 0.7 + 0.6 * jnp.arange(TOKENS, dtype=jnp.float32) / TOKENS
    return base * ramp[:, None]


def draw_key_states(key, part):
    scaled = shared_keys(key)
    result = scaled
    return result.astype(jnp.bfloat16)


def draw_queries(key, part):
    key = jax.random.fold_in(key, 7)
    own = jnp.clip(jax.random.normal(key, (TOKENS, HEADS * HD), jnp.float32), -6.0, 6.0)
    result = own
    return result.astype(jnp.bfloat16)


def draw_block_index(key, part):
    key = jax.random.fold_in(key, 3)
    per_owner = TOK_DEV // BLK
    ranking = jax.random.randint(key, (N_SEQ, per_owner), 0, 1 << 20) * per_owner + jnp.arange(per_owner, dtype=jnp.int32)[None, :]
    ordered = jnp.argsort(ranking, axis=1, stable=True)
    return ordered[:, :MB_DEV].astype(jnp.int32)


def block_levels(rng, dims, cuts, low, high):
    level = 1.0
    for position, shards_of in cuts:
        steps = jax.random.uniform(jax.random.fold_in(jax.random.fold_in(rng, 6), position), (shards_of,), jnp.float32, low / len(cuts), high / len(cuts))
        level = level * jnp.repeat(jnp.exp(steps), dims[position] // shards_of).reshape((-1,) + (1,) * (len(dims) - 1 - position))
    return level


def length_profile(amount, total, bound, slope):
    portions = [(1 << 20) // math.isqrt(standing ** slope) + 1 for standing in range(2, amount + 1)]
    surplus, holding = total - bound - (amount - 1), [1] * (amount - 1)
    while surplus > 0:
        movable = [i for i in range(amount - 1) if holding[i] < bound]
        pool, remaining = sum([portions[i] for i in movable]), surplus
        for i in movable:
            more = min(bound - holding[i], max(1, remaining * portions[i] // pool), surplus)
            holding[i] = holding[i] + more
            surplus = surplus - more
    return np.array([bound] + holding)


def ragged_sizes(stream_key, amount, total, most, lean):
    if amount == 2:
        one = jax.random.randint(stream_key, (), max(1, total - most), min(most, total - 1) + 1)
        return jnp.stack([one, total - one])
    tallies = jnp.asarray(length_profile(amount, total, most, lean), jnp.int32)
    couples = (amount - 1) // 2
    source_of, receiver = tallies[1:1 + 2 * couples:2], tallies[2:2 + 2 * couples:2]
    room = jnp.minimum(source_of - 1, most - receiver)
    passed = jax.random.randint(jax.random.fold_in(stream_key, 1), (couples,), 0, 1 << 20) % (room + 1)
    tallies = tallies.at[1:1 + 2 * couples:2].set(source_of - passed).at[2:2 + 2 * couples:2].set(receiver + passed)
    return tallies[jax.random.permutation(jax.random.fold_in(stream_key, 2), amount)]


def normal_values(key, shape, deviation, bound, cuts=(), kind=jnp.bfloat16):
    values = deviation * jax.random.normal(key, shape, jnp.float32)
    if cuts:
        values = values * block_levels(key, shape, cuts, -0.22, 0.18)
    return jnp.clip(values, -bound, bound).astype(kind)


def setup_inputs(seed: int = 0) -> dict:
    seeds = jax.random.split(jax.random.key(seed), 8)
    return {
        "queries": draw_queries(jax.random.fold_in(seeds[7], 71), 0),
        "key_states": draw_key_states(jax.random.fold_in(seeds[7], 71), 0),
        "value_states": normal_values(seeds[2], (TOKENS, HEADS * HD), 1.0, 6.0, ((0, 128), (1, 4))),
        "attn_output": normal_values(seeds[3], (TOKENS, HEADS * HD), 1.0, 6.0, ((0, 128), (1, 4))),
        "grad_output": normal_values(seeds[4], (TOKENS, HEADS * HD), 1.0, 6.0, ((0, 128), (1, 4))),
        "block_index": draw_block_index(jax.random.fold_in(seeds[7], 71), 0),
        "valid_count": ragged_sizes(seeds[6], N_SEQ, VALID_BLOCKS, MB_DEV, 2).astype(jnp.int32),
    }


def head_grads(pieces):
    query_head, grad_head, key_head, value_head, delta_head = pieces
    score_scale = HD ** -0.5
    scores = jnp.dot(query_head, key_head.T, preferred_element_type=jnp.float32) * score_scale
    peak = jnp.max(scores, axis=1, keepdims=True)
    log_total = peak + jnp.log(jnp.sum(jnp.exp(scores - peak), axis=1, keepdims=True))
    weights = jnp.exp(scores - log_total)
    weights_low = weights.astype(jnp.bfloat16)
    grad_value = jnp.dot(weights_low.T, grad_head, preferred_element_type=jnp.float32)
    dprobs = jnp.dot(grad_head, value_head.T, preferred_element_type=jnp.float32)
    dscores = (weights * (dprobs - delta_head[:, None])).astype(jnp.bfloat16)
    grad_query = jnp.dot(dscores, key_head, preferred_element_type=jnp.float32) * score_scale
    grad_key = jnp.dot(dscores.T, query_head, preferred_element_type=jnp.float32) * score_scale
    return grad_query, grad_key, grad_value


def split_heads(array_in, row_count):
    return array_in.reshape(row_count, HEADS, HD).transpose(1, 0, 2)


def merge_heads(array_in, row_count):
    return array_in.transpose(1, 0, 2).reshape(row_count, HEADS * HD)


def reference(queries, key_states, value_states, attn_output, grad_output, block_index, valid_count):
    live = jnp.arange(MB_DEV, dtype=jnp.int32)[None, :] < valid_count[:, None]
    order = jnp.argsort(jnp.where(live, 0, 1).astype(jnp.int32).reshape(-1), stable=True)[:VALID_BLOCKS]
    starts = (jnp.arange(N_SEQ, dtype=jnp.int32)[:, None] * TOK_DEV + block_index * BLK).reshape(-1)[order]
    row_ids = (starts[:, None] + jnp.arange(BLK, dtype=jnp.int32)[None, :]).reshape(-1).astype(jnp.int32)
    count_rows = VALID_BLOCKS * BLK
    picked_q = queries[row_ids]
    picked_g = grad_output[row_ids]
    picked_o = attn_output[row_ids]
    products = picked_g.astype(jnp.float32).reshape(count_rows, HEADS, HD) * picked_o.astype(jnp.float32).reshape(count_rows, HEADS, HD)
    row_delta = jnp.sum(products, axis=2).astype(jnp.bfloat16)
    grad_q, grad_k, grad_v = lax.map(head_grads, (split_heads(picked_q, count_rows), split_heads(picked_g, count_rows), split_heads(key_states, TOKENS), split_heads(value_states, TOKENS), row_delta.astype(jnp.float32).T))
    grad_queries = jnp.zeros((TOKENS, HEADS * HD), jnp.bfloat16).at[row_ids].set(merge_heads(grad_q, count_rows).astype(jnp.bfloat16))
    return grad_queries, merge_heads(grad_k, TOKENS).astype(jnp.bfloat16), merge_heads(grad_v, TOKENS).astype(jnp.bfloat16)
```

```python
import functools

import jax
import jax.numpy as jnp
from jax import lax
from jax.experimental import pallas as pl
from jax.experimental.pallas import tpu as pltpu
from jax.sharding import PartitionSpec as P

HD = 128
BLK = 4
MB_DEV = 4
HL = 3
FEAT = HL * HD
SLOTS = MB_DEV * BLK
TOK = 128
WIDE = 2 * FEAT + HD
KEYS = 4 * TOK
SCALE = HD ** (-0.5)
LOG2E = 1.4426950408889634
MESH = pl.DeviceIdType.MESH
NT = (((1,), (1,)), ((), ()))
NN = (((1,), (0,)), ((), ()))


def mm(a, b, dims):
    return lax.dot_general(a, b, dims, preferred_element_type=jnp.float32)


def cols(hh):
    return slice(hh * HD, (hh + 1) * HD)


def kernel(
    X, Y, H,
    bi_ref, vc_ref, q_ref, k_ref, v_ref, o_ref, g_ref,
    gq_ref, gk_ref, gv_ref,
    gbuf, kbuf, vbuf, kt, ebuf, dbuf, dqt, mrow, frow, srow, srow2, sxb, syb,
    dqs, rxb, dqo, dys, ryb, dqf, gpart, crecv, fsend, frecv,
    ysend, yrecv, xsend, xrecv, kvsend, kvrecv, ssx, srx, ssy, sry,
    dxs, dxr, dss, dsr, css, csr, fss, fsr, hss, hsr,
):
    C = Y * SLOTS
    s = lax.axis_index("seq")
    h = lax.axis_index("head")
    c = lax.rem(s, 2)
    x = lax.rem(s // 2, X)
    y = lax.rem(s // (2 * X), Y)
    z = s // (2 * X * Y)

    def dev(z_, y_, x_, c_, h_):
        return {"seq": ((z_ * Y + y_) * X + x_) * 2 + c_, "head": h_}

    def up(v, d, n):
        return lax.rem(v + d, n)

    def dn(v, d, n):
        return lax.rem(v + n - d, n)

    quad = [(0, 1), (1, 0), (1, 1)]
    final = [(dz, dh) for dz in range(2) for dh in range(H) if dz or dh]
    xp = [dev(z, y, up(x, e, X), c, h) for e in range(1, X)]
    yp = [dev(z, up(y, d, Y), x, c, h) for d in range(1, Y)]
    qp = [dev(up(z, dz, 2), y, x, up(c, dc, 2), h) for dz, dc in quad]
    fp = [dev(up(z, dz, 2), y, x, c, up(h, dh, H)) for dz, dh in final]
    extra = [p for p, (dz, dh) in zip(fp, final) if dh]

    barrier = pltpu.get_barrier_semaphore()
    greet = xp + yp + qp + extra
    for p in greet:
        pl.semaphore_signal(barrier, inc=1, device_id=p, device_id_type=MESH)

    def rcopy(src, dst, ss, rs, to):
        return pltpu.make_async_remote_copy(
            src_ref=src, dst_ref=dst, send_sem=ss, recv_sem=rs,
            device_id=to, device_id_type=MESH,
        )

    count = vc_ref[0] * BLK
    b = [bi_ref[0, j] * BLK for j in range(MB_DEV)]

    def targets(idx):
        j = idx // BLK
        t = jnp.where(j == 0, b[0], jnp.where(j == 1, b[1], jnp.where(j == 2, b[2], b[3])))
        return jnp.where(idx < count, t + lax.rem(idx, BLK), -1)

    ri = lax.broadcasted_iota(jnp.int32, (SLOTS, TOK), 0)
    li = lax.broadcasted_iota(jnp.int32, (SLOTS, TOK), 1)
    sel = jnp.where(targets(ri) == li, 1.0, 0.0).astype(jnp.bfloat16)
    own_q = mm(sel, q_ref[...], NN).astype(jnp.bfloat16)
    own_g = mm(sel, g_ref[...], NN)
    own_o = mm(sel, o_ref[...], NN)
    prod = own_g * own_o
    dcol = jnp.zeros((SLOTS, HD), jnp.float32)
    for hh in range(HL):
        dcol = jnp.where(li == hh, jnp.sum(prod[:, cols(hh)], axis=1, keepdims=True), dcol)
    gbuf[0, 0] = jnp.concatenate(
        [own_q, own_g.astype(jnp.bfloat16), dcol.astype(jnp.bfloat16)], axis=1
    )
    kbuf[0] = k_ref[...]
    vbuf[0] = v_ref[...]

    pl.semaphore_wait(barrier, len(greet))

    ysent = []
    for d in [Y // 2] + [t for i in range(1, (Y + 1) // 2) for t in (i, Y - i)]:
        cp = rcopy(gbuf.at[0, 0], gbuf.at[0, d], ysend.at[d - 1], yrecv.at[d - 1], yp[d - 1])
        cp.start()
        ysent.append(cp)
    kvsent = []
    for i, (src, buf) in enumerate(((k_ref, kbuf), (v_ref, vbuf))):
        for j in range(3):
            cp = rcopy(src, buf.at[j + 1], kvsend.at[i, j], kvrecv.at[i, j], qp[j])
            cp.start()
            kvsent.append(cp)
    xsent = []
    order = [0] + [t for i in range(1, (Y + 1) // 2) for t in (i, Y - i)] + [Y // 2]
    for d in order:
        if d:
            rcopy(gbuf.at[0, 0], gbuf.at[0, d], ysend.at[d - 1], yrecv.at[d - 1], yp[d - 1]).wait_recv()
        for e in range(1, X):
            cp = rcopy(gbuf.at[0, d], gbuf.at[e, d], xsend.at[d, e - 1], xrecv.at[d, e - 1], xp[e - 1])
            cp.start()
            xsent.append(cp)

    def kv_wait(i, buf):
        for j in range(3):
            rcopy(k_ref, buf.at[j + 1], kvsend.at[i, j], kvrecv.at[i, j], qp[j]).wait_recv()

    kv_wait(0, kbuf)
    for hh in range(HL):
        kt[hh] = kbuf[:, :, cols(hh)].reshape(KEYS, HD).T

    mrow[...] = jnp.zeros_like(mrow)
    srow[...] = jnp.zeros_like(srow)
    arrive = [0] + [e for e in range(1, X) if e != 2] + ([2] if X > 2 else [])
    for e in arrive:
        if e:
            for d in order:
                rcopy(gbuf.at[0, d], gbuf.at[e, d], xsend.at[d, e - 1], xrecv.at[d, e - 1], xp[e - 1]).wait_recv()
        for hh in range(HL):
            kh = kbuf[:, :, cols(hh)].reshape(KEYS, HD)
            qh = gbuf[e, :, :, cols(hh)].reshape(C, HD)
            s2 = mm(kh, qh, NT) * (SCALE * LOG2E)
            m = jnp.max(s2, axis=0, keepdims=True)
            ex = jnp.exp2(s2 - m)
            tot = jnp.sum(ex, axis=0, keepdims=True)
            ebuf[e, hh] = ex
            n = e * HL + hh
            mrow[n : n + 1, :] = m
            srow[n : n + 1, :] = m + jnp.log2(tot)

    def combine(parts):
        top = functools.reduce(jnp.maximum, parts)
        return top + jnp.log2(sum(jnp.exp2(p - top) for p in parts))

    stat_sent = []
    for e in range(1, X):
        cp = rcopy(srow, sxb.at[e - 1], ssx.at[e - 1], srx.at[e - 1], xp[e - 1])
        cp.start()
        stat_sent.append(cp)

    def dprobs(e):
        for hh in range(HL):
            vh = vbuf[:, :, cols(hh)].reshape(KEYS, HD)
            lane = lax.broadcasted_iota(jnp.int32, (KEYS, HD), 1)
            neg = jnp.where(lane == hh, -1.0, 0.0).astype(jnp.bfloat16)
            gh = gbuf[e, :, :, FEAT + hh * HD : FEAT + (hh + 1) * HD].reshape(C, HD)
            dh = gbuf[e, :, :, 2 * FEAT : WIDE].reshape(C, HD)
            dp = mm(jnp.concatenate([vh, neg], 1), jnp.concatenate([gh, dh], 1), NT)
            dd = ebuf[e, hh] * dp
            dbuf[e, hh] = dd
            dqt[e, hh] = mm(kt[hh], dd.astype(jnp.bfloat16), NN)

    kv_wait(1, vbuf)
    dprobs(0)
    if X > 2:
        dprobs(1)
    for e in range(1, X):
        cp = stat_sent[e - 1]
        cp.wait_recv()
    srow2[...] = srow[...]
    for i in range(X):
        parts = [srow[i * HL : (i + 1) * HL, :]]
        for e in range(1, X):
            n = (i - e) % X * HL
            parts.append(sxb[e - 1, n : n + HL, :])
        srow2[i * HL : (i + 1) * HL, :] = combine(parts)
    for d in range(1, Y):
        cp = rcopy(srow2, syb.at[d - 1], ssy.at[d - 1], sry.at[d - 1], yp[d - 1])
        cp.start()
        stat_sent.append(cp)
    for i in range(2 if X > 2 else 1, X):
        dprobs(i)
    for cp in stat_sent[X - 1 :]:
        cp.wait_recv()
    parts = [srow2[...]] + [pltpu.roll(syb[d - 1], d * SLOTS, 1) for d in range(1, Y)]
    frow[...] = jnp.exp2(mrow[...] - combine(parts))

    dq_sent = []
    for e in ([2] if X > 2 else []) + [e for e in range(1, X) if e != 2] + [0]:
        for hh in range(HL):
            n = e * HL + hh
            t = (dqt[e, hh] * (frow[n : n + 1, :] * SCALE)).T
            if e:
                dqs[e - 1, :, cols(hh)] = t.astype(jnp.bfloat16)
            else:
                dqo[:, cols(hh)] = t
        if e:
            cp = rcopy(dqs.at[e - 1], rxb.at[e - 1], dxs.at[e - 1], dxr.at[e - 1], xp[X - e - 1])
            cp.start()
            dq_sent.append(cp)

    core = dev(z, y, x, 1 - c, h)
    last_sent = []

    def grads(hh):
        f = [frow[i * HL + hh : i * HL + hh + 1, :] for i in range(X)]
        w = jnp.concatenate([(ebuf[i, hh] * f[i]).astype(jnp.bfloat16) for i in range(X)], axis=1)
        gvp = mm(w, gbuf[:, :, :, FEAT + hh * HD : FEAT + (hh + 1) * HD].reshape(X * C, HD), NN)
        ds = jnp.concatenate([(dbuf[i, hh] * f[i]).astype(jnp.bfloat16) for i in range(X)], axis=1)
        gkp = mm(ds, gbuf[:, :, :, cols(hh)].reshape(X * C, HD), NN) * SCALE
        for a, val in enumerate((gkp, gvp)):
            for i in range(4):
                gpart[hh, i % 2, a, i // 2] = val[i * TOK : (i + 1) * TOK].astype(jnp.bfloat16)
        cp = rcopy(gpart.at[hh, 1], crecv.at[hh], css.at[hh], csr.at[hh], core)
        cp.start()
        return cp

    def spread(hh, cp):
        cp.wait_recv()
        for a in range(2):
            for i in range(2):
                tot = gpart[hh, 0, a, i].astype(jnp.float32) + crecv[hh, a, i].astype(jnp.float32)
                fsend[hh, i, :, a] = tot.astype(jnp.bfloat16).reshape(H, TOK // H, HD)
        for n, (dz, dh) in enumerate(final):
            out = rcopy(
                fsend.at[hh, dz, up(h, dh, H)], frecv.at[hh, dz, h],
                fss.at[hh, n], fsr.at[hh, n], fp[n],
            )
            out.start()
            last_sent.append(out)
        frecv[hh, 0, h] = fsend[hh, 0, h]

    c0 = grads(0)
    for cp in dq_sent:
        cp.wait_recv()
    tot = dqo[...]
    for e in range(1, X):
        tot = tot + rxb[e - 1].astype(jnp.float32)
    dys[...] = tot.astype(jnp.bfloat16).reshape(Y, SLOTS, FEAT)
    y_sent = []
    for d in range(1, Y):
        cp = rcopy(dys.at[d], ryb.at[d - 1], dss.at[d - 1], dsr.at[d - 1], yp[Y - d - 1])
        cp.start()
        y_sent.append(cp)
    spread(0, c0)
    c1 = grads(1)
    spread(1, c1)
    for cp in y_sent:
        cp.wait_recv()
    tot = dys[0].astype(jnp.float32)
    for d in range(1, Y):
        tot = tot + ryb[d - 1].astype(jnp.float32)
    dqf[h] = tot.astype(jnp.bfloat16)
    head_sent = []
    for dh in range(1, H):
        to = dev(z, y, x, c, up(h, dh, H))
        cp = rcopy(dqf.at[h], dqf.at[h], hss.at[dh - 1], hsr.at[dh - 1], to)
        cp.start()
        head_sent.append(cp)
    c2 = grads(2)
    spread(2, c2)

    for dh in range(1, H):
        slot = dn(h, dh, H)
        rcopy(dqf.at[slot], dqf.at[slot], hss.at[dh - 1], hsr.at[dh - 1], xp[0]).wait_recv()
    out_rows = TOK // H
    pr = lax.broadcasted_iota(jnp.int32, (out_rows, SLOTS), 0) + h * out_rows
    pj = lax.broadcasted_iota(jnp.int32, (out_rows, SLOTS), 1)
    put = jnp.where(targets(pj) == pr, 1.0, 0.0).astype(jnp.bfloat16)
    for i in range(H):
        gq_ref[:, i * FEAT : (i + 1) * FEAT] = mm(put, dqf[i], NN).astype(jnp.bfloat16)
    for hh in range(HL):
        for n, (dz, dh) in enumerate(final):
            rcopy(
                fsend.at[hh, 0, 0], frecv.at[hh, dz, dn(h, dh, H)],
                fss.at[hh, n], fsr.at[hh, n], fp[n],
            ).wait_recv()
        for i in range(H):
            lanes = slice(i * FEAT + hh * HD, i * FEAT + (hh + 1) * HD)
            for a, ref in enumerate((gk_ref, gv_ref)):
                both = frecv[hh, 0, i, a].astype(jnp.float32) + frecv[hh, 1, i, a].astype(jnp.float32)
                ref[:, lanes] = both.astype(jnp.bfloat16)
    for cp in ysent + kvsent + xsent + stat_sent + dq_sent + [c0, c1, c2] + y_sent + head_sent + last_sent:
        cp.wait_send()


def body(X, Y, H, queries, key_states, value_states, attn_output, grad_output, block_index, valid_count):
    C = Y * SLOTS
    bf, f32 = jnp.bfloat16, jnp.float32
    V = pltpu.VMEM
    D = pltpu.SemaphoreType.DMA
    nf = 2 * H - 1
    scratch = [
        V((X, Y, SLOTS, WIDE), bf),
        V((4, TOK, FEAT), bf),
        V((4, TOK, FEAT), bf),
        V((HL, HD, KEYS), bf),
        V((X, HL, KEYS, C), f32),
        V((X, HL, KEYS, C), f32),
        V((X, HL, HD, C), f32),
        V((16, C), f32),
        V((16, C), f32),
        V((16, C), f32),
        V((16, C), f32),
        V((X - 1, 16, C), f32),
        V((Y - 1, 16, C), f32),
        V((X - 1, C, FEAT), bf),
        V((X - 1, C, FEAT), bf),
        V((C, FEAT), f32),
        V((Y, SLOTS, FEAT), bf),
        V((Y - 1, SLOTS, FEAT), bf),
        V((H, SLOTS, FEAT), bf),
        V((HL, 2, 2, 2, TOK, HD), bf),
        V((HL, 2, 2, TOK, HD), bf),
        V((HL, 2, H, 2, TOK // H, HD), bf),
        V((HL, 2, H, 2, TOK // H, HD), bf),
        D((Y - 1,)), D((Y - 1,)),
        D((Y, X - 1)), D((Y, X - 1)),
        D((2, 3)), D((2, 3)),
        D((X - 1,)), D((X - 1,)),
        D((Y - 1,)), D((Y - 1,)),
        D((X - 1,)), D((X - 1,)),
        D((Y - 1,)), D((Y - 1,)),
        D((HL,)), D((HL,)),
        D((HL, nf)), D((HL, nf)),
        D((H - 1,)), D((H - 1,)),
    ]
    out = jax.ShapeDtypeStruct((TOK // H, H * FEAT), bf)
    vm = pl.BlockSpec(memory_space=pltpu.VMEM)
    sm = pl.BlockSpec(memory_space=pltpu.SMEM)
    return pl.pallas_call(
        functools.partial(kernel, X, Y, H),
        out_shape=(out, out, out),
        in_specs=[sm, sm, vm, vm, vm, vm, vm],
        out_specs=(vm, vm, vm),
        scratch_shapes=scratch,
        compiler_params=pltpu.CompilerParams(
            collective_id=0, has_side_effects=True, vmem_limit_bytes=48 * 1024 * 1024
        ),
    )(block_index, valid_count, queries, key_states, value_states, attn_output, grad_output)


def build(mesh, X, Y):
    H = mesh.shape["head"]
    in_specs = tuple([P("seq", "head")] * 5) + (P("seq", None), P("seq"))
    out_specs = tuple([P(("seq", "head"), None)] * 3)
    return jax.shard_map(
        functools.partial(body, X, Y, H),
        mesh=mesh, in_specs=in_specs, out_specs=out_specs, check_vma=False,
    )


def solution(mesh):
    return build(mesh, 4, 8)
```

```python
import functools

import jax
import jax.numpy as jnp
from jax import lax
from jax.experimental import pallas as pl
from jax.experimental.pallas import tpu as pltpu
from jax.sharding import PartitionSpec as P

HD = 128
BLK = 4
MB_DEV = 4
HL = 3
FEAT = HL * HD
SLOTS = MB_DEV * BLK
TOK = 128
WIDE = FEAT + HD
KEYS = 4 * TOK
SCALE = HD ** (-0.5)
LOG2E = 1.4426950408889634
MESH = pl.DeviceIdType.MESH
NT = (((1,), (1,)), ((), ()))
NN = (((1,), (0,)), ((), ()))


def mm(a, b, dims):
    return lax.dot_general(a, b, dims, preferred_element_type=jnp.float32)


def cols(hh):
    return slice(hh * HD, (hh + 1) * HD)


def kernel(
    X, Y, H,
    bi_ref, vc_ref, q_hbm, k_ref, v_ref, o_hbm, g_hbm,
    gq_ref, gk_ref, gv_ref,
    q_ref, o_ref, g_ref,
    qbuf, gbuf, kbuf, vbuf, kt, ebuf, dbuf, dqt, mrow, frow, fxrow, srow, srow2, sxb, syb,
    dqs, rxb, dqo, dys, ryb, dqf, gpart, crecv, fsend, frecv,
    ysend, yrecv, xsend, xrecv, kvsend, kvrecv, ssx, srx, ssy, sry,
    dxs, dxr, dss, dsr, css, csr, fss, fsr, hss, hsr, lsem,
):
    C = Y * SLOTS
    s = lax.axis_index("seq")
    h = lax.axis_index("head")
    c = lax.rem(s, 2)
    x = lax.rem(s // 2, X)
    y = lax.rem(s // (2 * X), Y)
    z = s // (2 * X * Y)

    def dev(z_, y_, x_, c_, h_):
        return {"seq": ((z_ * Y + y_) * X + x_) * 2 + c_, "head": h_}

    def up(v, d, n):
        return lax.rem(v + d, n)

    def dn(v, d, n):
        return lax.rem(v + n - d, n)

    quad = [(0, 1), (1, 0), (1, 1)]
    final = [(dz, dh) for dz in range(2) for dh in range(H) if dz or dh]
    xp = [dev(z, y, up(x, e, X), c, h) for e in range(1, X)]
    yp = [dev(z, up(y, d, Y), x, c, h) for d in range(1, Y)]
    qp = [dev(up(z, dz, 2), y, x, up(c, dc, 2), h) for dz, dc in quad]
    fp = [dev(up(z, dz, 2), y, x, c, up(h, dh, H)) for dz, dh in final]
    extra = [p for p, (dz, dh) in zip(fp, final) if dh]

    barrier = pltpu.get_barrier_semaphore()
    greet = xp + yp + qp + extra
    for p in greet:
        pl.semaphore_signal(barrier, inc=1, device_id=p, device_id_type=MESH)

    local = [
        pltpu.make_async_copy(a, b, lsem.at[i])
        for i, (a, b) in enumerate((
            (q_hbm, q_ref), (g_hbm, g_ref), (o_hbm, o_ref), (k_ref, kbuf.at[0]), (v_ref, vbuf.at[0]),
        ))
    ]
    for cp in local:
        cp.start()

    def rcopy(src, dst, ss, rs, to):
        return pltpu.make_async_remote_copy(
            src_ref=src, dst_ref=dst, send_sem=ss, recv_sem=rs,
            device_id=to, device_id_type=MESH,
        )

    count = vc_ref[0] * BLK
    b = [bi_ref[0, j] * BLK for j in range(MB_DEV)]

    def targets(idx):
        j = idx // BLK
        t = jnp.where(j == 0, b[0], jnp.where(j == 1, b[1], jnp.where(j == 2, b[2], b[3])))
        return jnp.where(idx < count, t + lax.rem(idx, BLK), -1)

    ri = lax.broadcasted_iota(jnp.int32, (SLOTS, TOK), 0)
    li = lax.broadcasted_iota(jnp.int32, (SLOTS, TOK), 1)
    sel = jnp.where(targets(ri) == li, 1.0, 0.0).astype(jnp.bfloat16)
    local[0].wait()
    qbuf[0, 0] = mm(sel, q_ref[...], NN).astype(jnp.bfloat16)
    pl.semaphore_wait(barrier, len(greet))

    near = [t for i in range(1, (Y + 1) // 2) for t in (i, Y - i)]
    xorder = ([2] if X > 2 else []) + [e for e in range(1, X) if e != 2]
    sent = []

    def begin(cp):
        cp.start()
        sent.append(cp)
        return cp

    def ycopy(i, d):
        buf = (qbuf, gbuf)[i]
        return rcopy(buf.at[0, 0], buf.at[0, d], ysend.at[i, d - 1], yrecv.at[i, d - 1], yp[d - 1])

    def xcopy(i, d, e):
        buf = (qbuf, gbuf)[i]
        return rcopy(buf.at[0, d], buf.at[e, d], xsend.at[i, d, e - 1], xrecv.at[i, d, e - 1], xp[e - 1])

    def kvcopy(i, j):
        src, buf = ((k_ref, kbuf), (v_ref, vbuf))[i]
        return rcopy(src, buf.at[j + 1], kvsend.at[i, j], kvrecv.at[i, j], qp[j])

    def forward(i, d):
        if d:
            ycopy(i, d).wait_recv()
        for e in xorder:
            begin(xcopy(i, d, e))

    for d in [Y // 2] + near:
        begin(ycopy(0, d))
    for e in xorder:
        begin(xcopy(0, 0, e))
    for j in (1, 2, 0):
        begin(kvcopy(0, j))
    local[1].wait()
    local[2].wait()
    own_g = mm(sel, g_ref[...], NN)
    prod = own_g * mm(sel, o_ref[...], NN)
    dcol = jnp.zeros((SLOTS, HD), jnp.float32)
    for hh in range(HL):
        dcol = jnp.where(li == hh, jnp.sum(prod[:, cols(hh)], axis=1, keepdims=True), dcol)
    gbuf[0, 0] = jnp.concatenate([own_g.astype(jnp.bfloat16), dcol.astype(jnp.bfloat16)], axis=1)
    for d in [Y // 2] + near:
        begin(ycopy(1, d))
    for j in (1, 2, 0):
        begin(kvcopy(1, j))
    order = near + [Y // 2]
    for d in order:
        forward(0, d)

    local[3].wait()
    for j in range(3):
        kvcopy(0, j).wait_recv()
    for hh in range(HL):
        kt[hh] = kbuf[:, :, cols(hh)].reshape(KEYS, HD).T

    mrow[...] = jnp.zeros_like(mrow)
    srow[...] = jnp.zeros_like(srow)
    arrive = [e for e in range(1, X) if e != 2] + ([2] if X > 2 else [])

    def score(e):
        for hh in range(HL):
            kh = kbuf[:, :, cols(hh)].reshape(KEYS, HD)
            qh = qbuf[e, :, :, cols(hh)].reshape(C, HD)
            s2 = mm(kh, qh, NT) * (SCALE * LOG2E)
            m = jnp.max(s2, axis=0, keepdims=True)
            ex = jnp.exp2(s2 - m)
            tot = jnp.sum(ex, axis=0, keepdims=True)
            ebuf[e, hh] = ex
            n = e * HL + hh
            mrow[n : n + 1, :] = m
            srow[n : n + 1, :] = m + jnp.log2(tot)

    def combine(parts):
        top = functools.reduce(jnp.maximum, parts)
        return top + jnp.log2(sum(jnp.exp2(p - top) for p in parts))

    score(0)
    for d in [0] + order:
        forward(1, d)
    for e in arrive:
        for d in [0] + order:
            xcopy(0, d, e).wait_recv()
        score(e)
    stat_x = [
        begin(rcopy(srow, sxb.at[e - 1], ssx.at[e - 1], srx.at[e - 1], xp[e - 1]))
        for e in range(1, X)
    ]

    def dprobs(e):
        for hh in range(HL):
            vh = vbuf[:, :, cols(hh)].reshape(KEYS, HD)
            lane = lax.broadcasted_iota(jnp.int32, (KEYS, HD), 1)
            neg = jnp.where(lane == hh, -1.0, 0.0).astype(jnp.bfloat16)
            gh = gbuf[e, :, :, cols(hh)].reshape(C, HD)
            dh = gbuf[e, :, :, FEAT:WIDE].reshape(C, HD)
            dp = mm(jnp.concatenate([vh, neg], 1), jnp.concatenate([gh, dh], 1), NT)
            dd = ebuf[e, hh] * dp
            dbuf[e, hh] = dd
            dqt[e, hh] = mm(kt[hh], dd.astype(jnp.bfloat16), NN)

    local[4].wait()
    for j in range(3):
        kvcopy(1, j).wait_recv()
    dprobs(0)
    for cp in stat_x:
        cp.wait_recv()
    srow2[...] = srow[...]
    for i in range(X):
        parts = [srow[i * HL : (i + 1) * HL, :]]
        for e in range(1, X):
            n = (i - e) % X * HL
            parts.append(sxb[e - 1, n : n + HL, :])
        srow2[i * HL : (i + 1) * HL, :] = combine(parts)
    stat_y = [
        begin(rcopy(srow2, syb.at[d - 1], ssy.at[d - 1], sry.at[d - 1], yp[d - 1]))
        for d in [Y // 2] + near
    ]
    fxrow[...] = jnp.exp2(mrow[...] - srow2[...])

    def scaled(e, hh):
        n = e * HL + hh
        return (dqt[e, hh] * (fxrow[n : n + 1, :] * SCALE)).T

    dq_x = []
    for e in arrive:
        for d in [0] + order:
            xcopy(1, d, e).wait_recv()
        dprobs(e)
        for hh in range(HL):
            dqs[e - 1, :, cols(hh)] = scaled(e, hh).astype(jnp.bfloat16)
        dq_x.append(
            begin(rcopy(dqs.at[e - 1], rxb.at[e - 1], dxs.at[e - 1], dxr.at[e - 1], xp[X - e - 1]))
        )
    for hh in range(HL):
        dqo[:, cols(hh)] = scaled(0, hh)
    for cp in stat_y:
        cp.wait_recv()
    parts = [srow2[...]] + [pltpu.roll(syb[d - 1], d * SLOTS, 1) for d in range(1, Y)]
    log_total = combine(parts)
    frow[...] = jnp.exp2(mrow[...] - log_total)
    fyt = jnp.exp2(srow2[...] - log_total).T

    core = dev(z, y, x, 1 - c, h)

    def grads(hh):
        f = [frow[i * HL + hh : i * HL + hh + 1, :] for i in range(X)]
        w = jnp.concatenate([(ebuf[i, hh] * f[i]).astype(jnp.bfloat16) for i in range(X)], axis=1)
        gvp = mm(w, gbuf[:, :, :, cols(hh)].reshape(X * C, HD), NN)
        ds = jnp.concatenate([(dbuf[i, hh] * f[i]).astype(jnp.bfloat16) for i in range(X)], axis=1)
        gkp = mm(ds, qbuf[:, :, :, cols(hh)].reshape(X * C, HD), NN) * SCALE
        for a, val in enumerate((gkp, gvp)):
            for i in range(4):
                gpart[hh, i % 2, a, i // 2] = val[i * TOK : (i + 1) * TOK].astype(jnp.bfloat16)
        return begin(rcopy(gpart.at[hh, 1], crecv.at[hh], css.at[hh], csr.at[hh], core))

    def spread(hh, cp):
        cp.wait_recv()
        for a in range(2):
            for i in range(2):
                tot = gpart[hh, 0, a, i].astype(jnp.float32) + crecv[hh, a, i].astype(jnp.float32)
                fsend[hh, i, :, a] = tot.astype(jnp.bfloat16).reshape(H, TOK // H, HD)
        for n, (dz, dh) in enumerate(final):
            begin(rcopy(
                fsend.at[hh, dz, up(h, dh, H)], frecv.at[hh, dz, h],
                fss.at[hh, n], fsr.at[hh, n], fp[n],
            ))
        frecv[hh, 0, h] = fsend[hh, 0, h]

    c0 = grads(0)
    c1 = grads(1)
    spread(0, c0)
    for cp in dq_x:
        cp.wait_recv()
    for hh in range(HL):
        tot = dqo[:, cols(hh)]
        for e in range(1, X):
            tot = tot + rxb[e - 1, :, cols(hh)].astype(jnp.float32)
        tot = (tot * fyt[:, hh : hh + 1]).astype(jnp.bfloat16)
        dys[:, :, cols(hh)] = tot.reshape(Y, SLOTS, HD)
    dq_y = [
        begin(rcopy(dys.at[d], ryb.at[d - 1], dss.at[d - 1], dsr.at[d - 1], yp[Y - d - 1]))
        for d in [Y // 2] + near
    ]
    spread(1, c1)
    c2 = grads(2)
    spread(2, c2)
    for cp in dq_y:
        cp.wait_recv()
    tot = dys[0].astype(jnp.float32)
    for d in range(1, Y):
        tot = tot + ryb[d - 1].astype(jnp.float32)
    dqf[h] = tot.astype(jnp.bfloat16)
    for dh in range(1, H):
        to = dev(z, y, x, c, up(h, dh, H))
        begin(rcopy(dqf.at[h], dqf.at[h], hss.at[dh - 1], hsr.at[dh - 1], to))

    for hh in range(HL):
        for n, (dz, dh) in enumerate(final):
            rcopy(
                fsend.at[hh, 0, 0], frecv.at[hh, dz, dn(h, dh, H)],
                fss.at[hh, n], fsr.at[hh, n], fp[n],
            ).wait_recv()
        for i in range(H):
            lanes = slice(i * FEAT + hh * HD, i * FEAT + (hh + 1) * HD)
            for a, ref in enumerate((gk_ref, gv_ref)):
                both = frecv[hh, 0, i, a].astype(jnp.float32) + frecv[hh, 1, i, a].astype(jnp.float32)
                ref[:, lanes] = both.astype(jnp.bfloat16)
    for dh in range(1, H):
        slot = dn(h, dh, H)
        rcopy(dqf.at[slot], dqf.at[slot], hss.at[dh - 1], hsr.at[dh - 1], xp[0]).wait_recv()
    out_rows = TOK // H
    pr = lax.broadcasted_iota(jnp.int32, (out_rows, SLOTS), 0) + h * out_rows
    pj = lax.broadcasted_iota(jnp.int32, (out_rows, SLOTS), 1)
    put = jnp.where(targets(pj) == pr, 1.0, 0.0).astype(jnp.bfloat16)
    for i in range(H):
        gq_ref[:, i * FEAT : (i + 1) * FEAT] = mm(put, dqf[i], NN).astype(jnp.bfloat16)
    for cp in sent:
        cp.wait_send()


def body(X, Y, H, queries, key_states, value_states, attn_output, grad_output, block_index, valid_count):
    C = Y * SLOTS
    bf, f32 = jnp.bfloat16, jnp.float32
    V = pltpu.VMEM
    D = pltpu.SemaphoreType.DMA
    nf = 2 * H - 1
    scratch = [
        V((TOK, FEAT), bf),
        V((TOK, FEAT), bf),
        V((TOK, FEAT), bf),
        V((X, Y, SLOTS, FEAT), bf),
        V((X, Y, SLOTS, WIDE), bf),
        V((4, TOK, FEAT), bf),
        V((4, TOK, FEAT), bf),
        V((HL, HD, KEYS), bf),
        V((X, HL, KEYS, C), f32),
        V((X, HL, KEYS, C), f32),
        V((X, HL, HD, C), f32),
        V((16, C), f32),
        V((16, C), f32),
        V((16, C), f32),
        V((16, C), f32),
        V((16, C), f32),
        V((X - 1, 16, C), f32),
        V((Y - 1, 16, C), f32),
        V((X - 1, C, FEAT), bf),
        V((X - 1, C, FEAT), bf),
        V((C, FEAT), f32),
        V((Y, SLOTS, FEAT), bf),
        V((Y - 1, SLOTS, FEAT), bf),
        V((H, SLOTS, FEAT), bf),
        V((HL, 2, 2, 2, TOK, HD), bf),
        V((HL, 2, 2, TOK, HD), bf),
        V((HL, 2, H, 2, TOK // H, HD), bf),
        V((HL, 2, H, 2, TOK // H, HD), bf),
        D((2, Y - 1)), D((2, Y - 1)),
        D((2, Y, X - 1)), D((2, Y, X - 1)),
        D((2, 3)), D((2, 3)),
        D((X - 1,)), D((X - 1,)),
        D((Y - 1,)), D((Y - 1,)),
        D((X - 1,)), D((X - 1,)),
        D((Y - 1,)), D((Y - 1,)),
        D((HL,)), D((HL,)),
        D((HL, nf)), D((HL, nf)),
        D((H - 1,)), D((H - 1,)),
        D((5,)),
    ]
    out = jax.ShapeDtypeStruct((TOK // H, H * FEAT), bf)
    vm = pl.BlockSpec(memory_space=pltpu.VMEM)
    hb = pl.BlockSpec(memory_space=pltpu.HBM)
    sm = pl.BlockSpec(memory_space=pltpu.SMEM)
    return pl.pallas_call(
        functools.partial(kernel, X, Y, H),
        out_shape=(out, out, out),
        in_specs=[sm, sm, hb, hb, hb, hb, hb],
        out_specs=(vm, vm, vm),
        scratch_shapes=scratch,
        compiler_params=pltpu.CompilerParams(
            collective_id=0, has_side_effects=True, vmem_limit_bytes=63 * 1024 * 1024
        ),
    )(block_index, valid_count, queries, key_states, value_states, attn_output, grad_output)


def build(mesh, X, Y):
    H = mesh.shape["head"]
    in_specs = tuple([P("seq", "head")] * 5) + (P("seq", None), P("seq"))
    out_specs = tuple([P(("seq", "head"), None)] * 3)
    return jax.shard_map(
        functools.partial(body, X, Y, H),
        mesh=mesh, in_specs=in_specs, out_specs=out_specs, check_vma=False,
    )


def solution(mesh):
    return build(mesh, 4, 8)
```

```python
import functools

import jax
import jax.numpy as jnp
from jax import lax
from jax.experimental import pallas as pl
from jax.experimental.pallas import tpu as pltpu
from jax.sharding import PartitionSpec as P

HD = 128
BLK = 4
MB_DEV = 4
HL = 3
FEAT = HL * HD
SLOTS = MB_DEV * BLK
TOK = 128
WIDE = FEAT + HD
KEYS = 4 * TOK
SCALE = HD ** (-0.5)
LOG2E = 1.4426950408889634
MESH = pl.DeviceIdType.MESH
NT = (((1,), (1,)), ((), ()))
NN = (((1,), (0,)), ((), ()))


def mm(a, b, dims):
    return lax.dot_general(a, b, dims, preferred_element_type=jnp.float32)


def cols(hh):
    return slice(hh * HD, (hh + 1) * HD)


def kernel(
    X, Y, H,
    bi_ref, vc_ref, q_hbm, k_ref, v_ref, o_hbm, g_hbm,
    parts_ref,
    q_ref, o_ref, g_ref,
    qbuf, gbuf, kbuf, vbuf, kt, ebuf, dbuf, dqt, mrow, frow, wrow, srow, srow2, sxb, sxl, syb,
    dqs, rxb, dqo, dys, ryb, dqf, gpart, crecv, fsend, frecv,
    ysend, yrecv, xsend, xrecv, kvsend, kvrecv, ssx, srx, slx, rlx, ssy, sry,
    dxs, dxr, dss, dsr, css, csr, fss, fsr, hss, hsr, lsem,
):
    C = Y * SLOTS
    s = lax.axis_index("seq")
    h = lax.axis_index("head")
    c = lax.rem(s, 2)
    x = lax.rem(s // 2, X)
    y = lax.rem(s // (2 * X), Y)
    z = s // (2 * X * Y)

    def dev(z_, y_, x_, c_, h_):
        return {"seq": ((z_ * Y + y_) * X + x_) * 2 + c_, "head": h_}

    def up(v, d, n):
        return lax.rem(v + d, n)

    def dn(v, d, n):
        return lax.rem(v + n - d, n)

    quad = [(0, 1), (1, 0), (1, 1)]
    final = [(dz, dh) for dz in range(2) for dh in range(H) if dz or dh]
    xp = [dev(z, y, up(x, e, X), c, h) for e in range(1, X)]
    yp = [dev(z, up(y, d, Y), x, c, h) for d in range(1, Y)]
    qp = [dev(up(z, dz, 2), y, x, up(c, dc, 2), h) for dz, dc in quad]
    fp = [dev(up(z, dz, 2), y, x, c, up(h, dh, H)) for dz, dh in final]
    extra = [p for p, (dz, dh) in zip(fp, final) if dh]

    barrier = pltpu.get_barrier_semaphore()
    greet = xp + yp + qp + extra
    for p in greet:
        pl.semaphore_signal(barrier, inc=1, device_id=p, device_id_type=MESH)

    local = [
        pltpu.make_async_copy(a, b, lsem.at[i])
        for i, (a, b) in enumerate((
            (q_hbm, q_ref), (g_hbm, g_ref), (o_hbm, o_ref), (k_ref, kbuf.at[0]), (v_ref, vbuf.at[0]),
        ))
    ]
    for cp in local:
        cp.start()

    def rcopy(src, dst, ss, rs, to):
        return pltpu.make_async_remote_copy(
            src_ref=src, dst_ref=dst, send_sem=ss, recv_sem=rs,
            device_id=to, device_id_type=MESH,
        )

    count = vc_ref[0] * BLK
    b = [bi_ref[0, j] * BLK for j in range(MB_DEV)]

    def targets(idx):
        j = idx // BLK
        t = jnp.where(j == 0, b[0], jnp.where(j == 1, b[1], jnp.where(j == 2, b[2], b[3])))
        return jnp.where(idx < count, t + lax.rem(idx, BLK), -1)

    ri = lax.broadcasted_iota(jnp.int32, (SLOTS, TOK), 0)
    li = lax.broadcasted_iota(jnp.int32, (SLOTS, TOK), 1)
    sel = jnp.where(targets(ri) == li, 1.0, 0.0).astype(jnp.bfloat16)
    local[0].wait()
    qbuf[0, 0] = mm(sel, q_ref[...], NN).astype(jnp.bfloat16)
    pl.semaphore_wait(barrier, len(greet))

    near = [t for i in range(1, (Y + 1) // 2) for t in (i, Y - i)]
    xorder = ([2] if X > 2 else []) + [e for e in range(1, X) if e != 2]
    sent = []

    def begin(cp):
        cp.start()
        sent.append(cp)
        return cp

    def ycopy(i, d):
        buf = (qbuf, gbuf)[i]
        return rcopy(buf.at[0, 0], buf.at[0, d], ysend.at[i, d - 1], yrecv.at[i, d - 1], yp[d - 1])

    def xcopy(i, d, e):
        buf = (qbuf, gbuf)[i]
        return rcopy(buf.at[0, d], buf.at[e, d], xsend.at[i, d, e - 1], xrecv.at[i, d, e - 1], xp[e - 1])

    def kvcopy(i, j):
        src, buf = ((k_ref, kbuf), (v_ref, vbuf))[i]
        return rcopy(src, buf.at[j + 1], kvsend.at[i, j], kvrecv.at[i, j], qp[j])

    for d in [Y // 2] + near:
        begin(ycopy(0, d))
    for e in xorder:
        begin(xcopy(0, 0, e))
    for j in (1, 2, 0):
        begin(kvcopy(0, j))
    local[1].wait()
    local[2].wait()
    own_g = mm(sel, g_ref[...], NN)
    prod = own_g * mm(sel, o_ref[...], NN)
    dcol = jnp.zeros((SLOTS, HD), jnp.float32)
    for hh in range(HL):
        dcol = jnp.where(li == hh, jnp.sum(prod[:, cols(hh)], axis=1, keepdims=True), dcol)
    gbuf[0, 0] = jnp.concatenate([own_g.astype(jnp.bfloat16), dcol.astype(jnp.bfloat16)], axis=1)
    for d in [Y // 2] + near:
        begin(ycopy(1, d))
    for j in (1, 2, 0):
        begin(kvcopy(1, j))
    order = near + [Y // 2]
    for d in order:
        ycopy(0, d).wait_recv()
        for e in xorder:
            begin(xcopy(0, d, e))
    for e in xorder:
        for d in [0] + order:
            if d and e == xorder[0]:
                ycopy(1, d).wait_recv()
            begin(xcopy(1, d, e))

    local[3].wait()
    for j in range(3):
        kvcopy(0, j).wait_recv()
    for hh in range(HL):
        kt[hh] = kbuf[:, :, cols(hh)].reshape(KEYS, HD).T

    mrow[...] = jnp.zeros_like(mrow)
    srow[...] = jnp.zeros_like(srow)
    arrive = [e for e in range(1, X) if e != 2] + ([2] if X > 2 else [])

    def score(e):
        for hh in range(HL):
            kh = kbuf[:, :, cols(hh)].reshape(KEYS, HD)
            qh = qbuf[e, :, :, cols(hh)].reshape(C, HD)
            s2 = mm(kh, qh, NT) * (SCALE * LOG2E)
            m = jnp.max(s2, axis=0, keepdims=True)
            ex = jnp.exp2(s2 - m)
            tot = jnp.sum(ex, axis=0, keepdims=True)
            ebuf[e, hh] = ex
            n = e * HL + hh
            mrow[n : n + 1, :] = m
            srow[n : n + 1, :] = m + jnp.log2(tot)

    def combine(parts):
        top = functools.reduce(jnp.maximum, parts)
        return top + jnp.log2(sum(jnp.exp2(p - top) for p in parts))

    score(0)
    for e in arrive:
        for d in [0] + order:
            xcopy(0, d, e).wait_recv()
        score(e)
    stat_y = [
        begin(rcopy(srow, syb.at[d - 1], ssy.at[d - 1], sry.at[d - 1], yp[d - 1]))
        for d in [Y // 2] + near
    ]
    stat_l = [
        begin(rcopy(srow, sxl.at[e - 1], slx.at[e - 1], rlx.at[e - 1], xp[e - 1]))
        for e in range(1, X)
    ]

    def dprobs(e):
        for hh in range(HL):
            vh = vbuf[:, :, cols(hh)].reshape(KEYS, HD)
            lane = lax.broadcasted_iota(jnp.int32, (KEYS, HD), 1)
            neg = jnp.where(lane == hh, -1.0, 0.0).astype(jnp.bfloat16)
            gh = gbuf[e, :, :, cols(hh)].reshape(C, HD)
            dh = gbuf[e, :, :, FEAT:WIDE].reshape(C, HD)
            dp = mm(jnp.concatenate([vh, neg], 1), jnp.concatenate([gh, dh], 1), NT)
            dd = ebuf[e, hh] * dp
            dbuf[e, hh] = dd
            dqt[e, hh] = mm(kt[hh], dd.astype(jnp.bfloat16), NN)

    local[4].wait()
    for j in range(3):
        kvcopy(1, j).wait_recv()

    def scaled(e, hh):
        n = e * HL + hh
        row = jnp.exp2(mrow[n : n + 1, :] - srow[n : n + 1, :])
        return (dqt[e, hh] * (row * SCALE)).T

    dq_x = []
    def send_dq(e):
        for d in [0] + order:
            xcopy(1, d, e).wait_recv()
        dprobs(e)
        for hh in range(HL):
            dqs[e - 1, :, cols(hh)] = scaled(e, hh).astype(jnp.bfloat16)
        dq_x.append(
            begin(rcopy(dqs.at[e - 1], rxb.at[e - 1], dxs.at[e - 1], dxr.at[e - 1], xp[X - e - 1]))
        )
    send_dq(xorder[0])
    dprobs(0)
    for hh in range(HL):
        dqo[:, cols(hh)] = scaled(0, hh)

    for cp in stat_y:
        cp.wait_recv()
    srow2[...] = combine([srow[...]] + [pltpu.roll(syb[d - 1], d * SLOTS, 1) for d in range(1, Y)])
    stat_x = [
        begin(rcopy(srow2, sxb.at[e - 1], ssx.at[e - 1], srx.at[e - 1], xp[e - 1]))
        for e in xorder
    ]
    for e in xorder[1:]:
        send_dq(e)
    for cp in stat_x + stat_l:
        cp.wait_recv()
    for i in range(X):
        rows = slice(i * HL, (i + 1) * HL)
        parts = [srow2[rows, :]]
        for e in range(1, X):
            n = (i - e) % X * HL
            parts.append(sxb[e - 1, n : n + HL, :])
        log_total = combine(parts)
        frow[rows, :] = jnp.exp2(mrow[rows, :] - log_total)
        if i == 0:
            wrow[...] = jnp.zeros_like(wrow)
            wrow[rows, :] = jnp.exp2(srow[rows, :] - log_total)
            for e in range(1, X):
                n = e * HL
                wrow[n : n + HL, :] = jnp.exp2(sxl[X - e - 1, n : n + HL, :] - log_total)

    core = dev(z, y, x, 1 - c, h)

    def grads(hh):
        f = [frow[i * HL + hh : i * HL + hh + 1, :] for i in range(X)]
        w = jnp.concatenate([(ebuf[i, hh] * f[i]).astype(jnp.bfloat16) for i in range(X)], axis=1)
        gvp = mm(w, gbuf[:, :, :, cols(hh)].reshape(X * C, HD), NN)
        ds = jnp.concatenate([(dbuf[i, hh] * f[i]).astype(jnp.bfloat16) for i in range(X)], axis=1)
        gkp = mm(ds, qbuf[:, :, :, cols(hh)].reshape(X * C, HD), NN) * SCALE
        for a, val in enumerate((gkp, gvp)):
            for i in range(4):
                gpart[hh, i % 2, a, i // 2] = val[i * TOK : (i + 1) * TOK].astype(jnp.bfloat16)
        return begin(rcopy(gpart.at[hh, 1], crecv.at[hh], css.at[hh], csr.at[hh], core))

    def spread(hh, cp):
        cp.wait_recv()
        for a in range(2):
            for i in range(2):
                tot = gpart[hh, 0, a, i].astype(jnp.float32) + crecv[hh, a, i].astype(jnp.float32)
                fsend[hh, i, :, a] = tot.astype(jnp.bfloat16).reshape(H, TOK // H, HD)
        for n, (dz, dh) in enumerate(final):
            begin(rcopy(
                fsend.at[hh, dz, up(h, dh, H)], frecv.at[hh, dz, h],
                fss.at[hh, n], fsr.at[hh, n], fp[n],
            ))
        frecv[hh, 0, h] = fsend[hh, 0, h]

    c0 = grads(0)
    c1 = grads(1)
    spread(0, c0)
    weight = wrow[...].T
    for cp in dq_x:
        cp.wait_recv()
    for hh in range(HL):
        tot = dqo[:, cols(hh)] * weight[:, hh : hh + 1]
        for e in range(1, X):
            n = e * HL + hh
            tot = tot + rxb[e - 1, :, cols(hh)].astype(jnp.float32) * weight[:, n : n + 1]
        dys[:, :, cols(hh)] = tot.astype(jnp.bfloat16).reshape(Y, SLOTS, HD)
    dq_y = [
        begin(rcopy(dys.at[d], ryb.at[d - 1], dss.at[d - 1], dsr.at[d - 1], yp[Y - d - 1]))
        for d in [Y // 2] + near
    ]
    spread(1, c1)
    c2 = grads(2)
    spread(2, c2)
    for cp in dq_y:
        cp.wait_recv()
    tot = dys[0].astype(jnp.float32)
    for d in range(1, Y):
        tot = tot + ryb[d - 1].astype(jnp.float32)
    dqf[h] = tot.astype(jnp.bfloat16)
    for dh in range(1, H):
        to = dev(z, y, x, c, up(h, dh, H))
        begin(rcopy(dqf.at[h], dqf.at[h], hss.at[dh - 1], hsr.at[dh - 1], to))

    for hh in range(HL):
        for n, (dz, dh) in enumerate(final):
            rcopy(
                fsend.at[hh, 0, 0], frecv.at[hh, dz, dn(h, dh, H)],
                fss.at[hh, n], fsr.at[hh, n], fp[n],
            ).wait_recv()
        for i in range(H):
            lanes = slice(i * FEAT + hh * HD, i * FEAT + (hh + 1) * HD)
            for a in range(2):
                for p in range(2):
                    parts_ref[p, a + 1, :, lanes] = frecv[hh, p, i, a]
    for dh in range(1, H):
        slot = dn(h, dh, H)
        rcopy(dqf.at[slot], dqf.at[slot], hss.at[dh - 1], hsr.at[dh - 1], xp[0]).wait_recv()
    out_rows = TOK // H
    pr = lax.broadcasted_iota(jnp.int32, (out_rows, SLOTS), 0) + h * out_rows
    pj = lax.broadcasted_iota(jnp.int32, (out_rows, SLOTS), 1)
    put = jnp.where(targets(pj) == pr, 1.0, 0.0).astype(jnp.bfloat16)
    for i in range(H):
        lanes = slice(i * FEAT, (i + 1) * FEAT)
        for p in range(2):
            half = jnp.where(pj // (SLOTS // 2) == p, put, jnp.zeros_like(put))
            parts_ref[p, 0, :, lanes] = mm(half, dqf[i], NN).astype(jnp.bfloat16)
    for cp in sent:
        cp.wait_send()


def body(X, Y, H, queries, key_states, value_states, attn_output, grad_output, block_index, valid_count):
    C = Y * SLOTS
    bf, f32 = jnp.bfloat16, jnp.float32
    V = pltpu.VMEM
    D = pltpu.SemaphoreType.DMA
    nf = 2 * H - 1
    scratch = [
        V((TOK, FEAT), bf),
        V((TOK, FEAT), bf),
        V((TOK, FEAT), bf),
        V((X, Y, SLOTS, FEAT), bf),
        V((X, Y, SLOTS, WIDE), bf),
        V((4, TOK, FEAT), bf),
        V((4, TOK, FEAT), bf),
        V((HL, HD, KEYS), bf),
        V((X, HL, KEYS, C), f32),
        V((X, HL, KEYS, C), f32),
        V((X, HL, HD, C), f32),
        V((16, C), f32),
        V((16, C), f32),
        V((16, C), f32),
        V((16, C), f32),
        V((16, C), f32),
        V((X - 1, 16, C), f32),
        V((X - 1, 16, C), f32),
        V((Y - 1, 16, C), f32),
        V((X - 1, C, FEAT), bf),
        V((X - 1, C, FEAT), bf),
        V((C, FEAT), f32),
        V((Y, SLOTS, FEAT), bf),
        V((Y - 1, SLOTS, FEAT), bf),
        V((H, SLOTS, FEAT), bf),
        V((HL, 2, 2, 2, TOK, HD), bf),
        V((HL, 2, 2, TOK, HD), bf),
        V((HL, 2, H, 2, TOK // H, HD), bf),
        V((HL, 2, H, 2, TOK // H, HD), bf),
        D((2, Y - 1)), D((2, Y - 1)),
        D((2, Y, X - 1)), D((2, Y, X - 1)),
        D((2, 3)), D((2, 3)),
        D((X - 1,)), D((X - 1,)),
        D((X - 1,)), D((X - 1,)),
        D((Y - 1,)), D((Y - 1,)),
        D((X - 1,)), D((X - 1,)),
        D((Y - 1,)), D((Y - 1,)),
        D((HL,)), D((HL,)),
        D((HL, nf)), D((HL, nf)),
        D((H - 1,)), D((H - 1,)),
        D((5,)),
    ]
    out = jax.ShapeDtypeStruct((TOK // H, H * FEAT), bf)
    parts = jax.ShapeDtypeStruct((2, 3, TOK // H, H * FEAT), bf)
    vm = pl.BlockSpec(memory_space=pltpu.VMEM)
    hb = pl.BlockSpec(memory_space=pltpu.HBM)
    sm = pl.BlockSpec(memory_space=pltpu.SMEM)
    parts = pl.pallas_call(
        functools.partial(kernel, X, Y, H),
        out_shape=parts,
        in_specs=[sm, sm, hb, hb, hb, hb, hb],
        out_specs=vm,
        scratch_shapes=scratch,
        compiler_params=pltpu.CompilerParams(
            collective_id=0, has_side_effects=True, vmem_limit_bytes=63 * 1024 * 1024
        ),
    )(block_index, valid_count, queries, key_states, value_states, attn_output, grad_output)
    return tuple(
        (parts[0, a].astype(f32) + parts[1, a].astype(f32)).astype(bf) for a in range(3)
    )


def build(mesh, X, Y):
    H = mesh.shape["head"]
    in_specs = tuple([P("seq", "head")] * 5) + (P("seq", None), P("seq"))
    out_specs = tuple([P(("seq", "head"), None)] * 3)
    return jax.shard_map(
        functools.partial(body, X, Y, H),
        mesh=mesh, in_specs=in_specs, out_specs=out_specs, check_vma=False,
    )


def solution(mesh):
    return build(mesh, 4, 8)
```

```python
import functools

import jax
import jax.numpy as jnp
from jax import lax
from jax.experimental import pallas as pl
from jax.experimental.pallas import tpu as pltpu
from jax.sharding import PartitionSpec as P

HD = 128
BLK = 4
MB_DEV = 4
HL = 3
FEAT = HL * HD
SLOTS = MB_DEV * BLK
TOK = 128
KEYS = 4 * TOK
SCALE = HD ** (-0.5)
LOG2E = 1.4426950408889634
MESH = pl.DeviceIdType.MESH
NT = (((1,), (1,)), ((), ()))
NN = (((1,), (0,)), ((), ()))
TN = (((0,), (0,)), ((), ()))


def mm(a, b, dims):
    return lax.dot_general(a, b, dims, preferred_element_type=jnp.float32)


def cols(hh):
    return slice(hh * HD, (hh + 1) * HD)


def kernel(
    X, Y, H,
    bi_ref, vc_ref, q_hbm, k_ref, v_ref, o_hbm, g_hbm,
    parts_ref,
    q_ref, o_ref, g_ref,
    qbuf, gbuf, dly, dlx, kbuf, vbuf, kt, ebuf, dbuf, dqt, mrow, frow, wrow, srow, srow2, sxb, sxl, syb,
    dqs, rxb, dqo, dys, ryb, dqf, gpart, crecv, fsend, frecv,
    dysend, dyrecv, dxsend, dxrecv, ysend, yrecv, xsend, xrecv, kvsend, kvrecv, ssx, srx, slx, rlx, ssy, sry,
    dxs, dxr, dss, dsr, css, csr, fss, fsr, hss, hsr, lsem,
):
    C = Y * SLOTS
    s = lax.axis_index("seq")
    h = lax.axis_index("head")
    c = lax.rem(s, 2)
    x = lax.rem(s // 2, X)
    y = lax.rem(s // (2 * X), Y)
    z = s // (2 * X * Y)

    def dev(z_, y_, x_, c_, h_):
        return {"seq": ((z_ * Y + y_) * X + x_) * 2 + c_, "head": h_}

    def up(v, d, n):
        return lax.rem(v + d, n)

    def dn(v, d, n):
        return lax.rem(v + n - d, n)

    quad = [(0, 1), (1, 0), (1, 1)]
    final = [(dz, dh) for dz in range(2) for dh in range(H) if dz or dh]
    final.sort(key=lambda t: abs(t[1] - H // 2))
    xp = [dev(z, y, up(x, e, X), c, h) for e in range(1, X)]
    yp = [dev(z, up(y, d, Y), x, c, h) for d in range(1, Y)]
    qp = [dev(up(z, dz, 2), y, x, up(c, dc, 2), h) for dz, dc in quad]
    fp = [dev(up(z, dz, 2), y, x, c, up(h, dh, H)) for dz, dh in final]
    extra = [p for p, (dz, dh) in zip(fp, final) if dh]

    barrier = pltpu.get_barrier_semaphore()
    greet = xp + yp + qp + extra
    for p in greet:
        pl.semaphore_signal(barrier, inc=1, device_id=p, device_id_type=MESH)

    local = [
        pltpu.make_async_copy(a, b, lsem.at[i])
        for i, (a, b) in enumerate((
            (q_hbm, q_ref), (g_hbm, g_ref), (o_hbm, o_ref), (k_ref, kbuf.at[0]), (v_ref, vbuf.at[0]),
        ))
    ]
    for cp in local:
        cp.start()

    def rcopy(src, dst, ss, rs, to):
        return pltpu.make_async_remote_copy(
            src_ref=src, dst_ref=dst, send_sem=ss, recv_sem=rs,
            device_id=to, device_id_type=MESH,
        )

    count = vc_ref[0] * BLK
    b = [bi_ref[0, j] * BLK for j in range(MB_DEV)]

    def targets(idx):
        j = idx // BLK
        t = jnp.where(j == 0, b[0], jnp.where(j == 1, b[1], jnp.where(j == 2, b[2], b[3])))
        return jnp.where(idx < count, t + lax.rem(idx, BLK), -1)

    ri = lax.broadcasted_iota(jnp.int32, (SLOTS, TOK), 0)
    li = lax.broadcasted_iota(jnp.int32, (SLOTS, TOK), 1)
    sel = jnp.where(targets(ri) == li, 1.0, 0.0).astype(jnp.bfloat16)
    local[0].wait()
    qbuf[0, 0] = mm(sel, q_ref[...], NN).astype(jnp.bfloat16)
    pl.semaphore_wait(barrier, len(greet))

    near = [t for i in range(1, (Y + 1) // 2) for t in (i, Y - i)]
    xorder = ([2] if X > 2 else []) + [e for e in range(1, X) if e != 2]
    sent = []

    def begin(cp):
        cp.start()
        sent.append(cp)
        return cp

    def ycopy(i, d):
        buf = (qbuf, gbuf)[i]
        return rcopy(buf.at[0, 0], buf.at[0, d], ysend.at[i, d - 1], yrecv.at[i, d - 1], yp[d - 1])

    def xcopy(i, d, e):
        buf = (qbuf, gbuf)[i]
        return rcopy(buf.at[0, d], buf.at[e, d], xsend.at[i, d, e - 1], xrecv.at[i, d, e - 1], xp[e - 1])

    def kvcopy(i, j):
        src, buf = ((k_ref, kbuf), (v_ref, vbuf))[i]
        return rcopy(src, buf.at[j + 1], kvsend.at[i, j], kvrecv.at[i, j], qp[j])

    for d in [Y // 2] + near:
        begin(ycopy(0, d))
    for e in xorder:
        begin(xcopy(0, 0, e))
    for j in (1, 2, 0):
        begin(kvcopy(0, j))
    local[1].wait()
    local[2].wait()
    own_g = mm(sel, g_ref[...], NN)
    prod = own_g * mm(sel, o_ref[...], NN)
    dcol = jnp.zeros((SLOTS, HD), jnp.float32)
    for hh in range(HL):
        dcol = jnp.where(li == hh, jnp.sum(prod[:, cols(hh)], axis=1, keepdims=True), dcol)
    gbuf[0, 0] = own_g.astype(jnp.bfloat16)
    ident = jnp.where(
        lax.broadcasted_iota(jnp.int32, (SLOTS, C), 0)
        == lax.broadcasted_iota(jnp.int32, (SLOTS, C), 1), 1.0, 0.0,
    ).astype(jnp.bfloat16)
    dly[0] = mm(dcol.astype(jnp.bfloat16), ident, TN)[:8]

    def dycopy(d):
        return rcopy(dly.at[0], dly.at[d], dysend.at[d - 1], dyrecv.at[d - 1], yp[d - 1])

    def dxcopy(e):
        return rcopy(dlx.at[0], dlx.at[e], dxsend.at[e - 1], dxrecv.at[e - 1], xp[e - 1])

    for d in [Y // 2] + near:
        begin(ycopy(1, d))
    for d in [Y // 2] + near:
        begin(dycopy(d))
    for j in (1, 2, 0):
        begin(kvcopy(1, j))
    order = near + [Y // 2]
    for d in order:
        ycopy(0, d).wait_recv()
        for e in xorder:
            begin(xcopy(0, d, e))
    for e in xorder:
        for d in [0] + order:
            if d and e == xorder[0]:
                ycopy(1, d).wait_recv()
            begin(xcopy(1, d, e))
    for d in order:
        dycopy(d).wait_recv()
    dlx[0] = sum([dly[0]] + [pltpu.roll(dly[d], d * SLOTS, 1) for d in range(1, Y)])
    for e in xorder:
        begin(dxcopy(e))

    local[3].wait()
    for j in range(3):
        kvcopy(0, j).wait_recv()
    for hh in range(HL):
        kt[hh] = kbuf[:, :, cols(hh)].reshape(KEYS, HD).T

    mrow[...] = jnp.zeros_like(mrow)
    srow[...] = jnp.zeros_like(srow)
    arrive = [e for e in range(1, X) if e != 2] + ([2] if X > 2 else [])

    def score(e):
        for hh in range(HL):
            kh = kbuf[:, :, cols(hh)].reshape(KEYS, HD)
            qh = qbuf[e, :, :, cols(hh)].reshape(C, HD)
            s2 = mm(kh, qh, NT) * (SCALE * LOG2E)
            m = jnp.max(s2, axis=0, keepdims=True)
            ex = jnp.exp2(s2 - m)
            tot = jnp.sum(ex, axis=0, keepdims=True)
            ebuf[e, hh] = ex
            n = e * HL + hh
            mrow[n : n + 1, :] = m
            srow[n : n + 1, :] = m + jnp.log2(tot)

    def combine(parts):
        top = functools.reduce(jnp.maximum, parts)
        return top + jnp.log2(sum(jnp.exp2(p - top) for p in parts))

    score(0)
    for e in arrive:
        for d in [0] + order:
            xcopy(0, d, e).wait_recv()
        score(e)
    stat_y = [
        begin(rcopy(srow, syb.at[d - 1], ssy.at[d - 1], sry.at[d - 1], yp[d - 1]))
        for d in [Y // 2] + near
    ]
    stat_l = [
        begin(rcopy(srow, sxl.at[e - 1], slx.at[e - 1], rlx.at[e - 1], xp[e - 1]))
        for e in range(1, X)
    ]

    def dprobs(e):
        for hh in range(HL):
            vh = vbuf[:, :, cols(hh)].reshape(KEYS, HD)
            gh = gbuf[e, :, :, cols(hh)].reshape(C, HD)
            dp = mm(vh, gh, NT) - dlx[e, hh : hh + 1, :]
            dd = ebuf[e, hh] * dp
            dbuf[e, hh] = dd
            dqt[e, hh] = mm(kt[hh], dd.astype(jnp.bfloat16), NN)

    local[4].wait()
    for j in range(3):
        kvcopy(1, j).wait_recv()

    def scaled(e, hh):
        n = e * HL + hh
        row = jnp.exp2(mrow[n : n + 1, :] - srow[n : n + 1, :])
        return (dqt[e, hh] * (row * SCALE)).T

    dq_x = []
    def make_dq(e):
        for d in [0] + order:
            xcopy(1, d, e).wait_recv()
        dxcopy(e).wait_recv()
        dprobs(e)
        for hh in range(HL):
            dqs[e - 1, :, cols(hh)] = scaled(e, hh).astype(jnp.bfloat16)

    def send_dq(e):
        dq_x.append(
            begin(rcopy(dqs.at[e - 1], rxb.at[e - 1], dxs.at[e - 1], dxr.at[e - 1], xp[X - e - 1]))
        )

    dprobs(0)
    for hh in range(HL):
        dqo[:, cols(hh)] = scaled(0, hh)
    make_dq(xorder[0])

    for cp in stat_y:
        cp.wait_recv()
    srow2[...] = combine([srow[...]] + [pltpu.roll(syb[d - 1], d * SLOTS, 1) for d in range(1, Y)])
    stat_x = [
        begin(rcopy(srow2, sxb.at[e - 1], ssx.at[e - 1], srx.at[e - 1], xp[e - 1]))
        for e in xorder
    ]
    send_dq(xorder[0])
    for e in xorder[1:]:
        make_dq(e)
        send_dq(e)
    for cp in stat_x + stat_l:
        cp.wait_recv()
    for i in range(X):
        rows = slice(i * HL, (i + 1) * HL)
        parts = [srow2[rows, :]]
        for e in range(1, X):
            n = (i - e) % X * HL
            parts.append(sxb[e - 1, n : n + HL, :])
        log_total = combine(parts)
        frow[rows, :] = jnp.exp2(mrow[rows, :] - log_total)
        if i == 0:
            wrow[...] = jnp.zeros_like(wrow)
            wrow[rows, :] = jnp.exp2(srow[rows, :] - log_total)
            for e in range(1, X):
                n = e * HL
                wrow[n : n + HL, :] = jnp.exp2(sxl[X - e - 1, n : n + HL, :] - log_total)

    core = dev(z, y, x, 1 - c, h)

    def grads(hh):
        f = [frow[i * HL + hh : i * HL + hh + 1, :] for i in range(X)]
        w = jnp.concatenate([(ebuf[i, hh] * f[i]).astype(jnp.bfloat16) for i in range(X)], axis=1)
        gvp = mm(w, gbuf[:, :, :, cols(hh)].reshape(X * C, HD), NN)
        ds = jnp.concatenate([(dbuf[i, hh] * f[i]).astype(jnp.bfloat16) for i in range(X)], axis=1)
        gkp = mm(ds, qbuf[:, :, :, cols(hh)].reshape(X * C, HD), NN) * SCALE
        for a, val in enumerate((gkp, gvp)):
            for i in range(4):
                gpart[hh, i % 2, a, i // 2] = val[i * TOK : (i + 1) * TOK].astype(jnp.bfloat16)
        return begin(rcopy(gpart.at[hh, 1], crecv.at[hh], css.at[hh], csr.at[hh], core))

    def spread(hh, cp):
        cp.wait_recv()
        for a in range(2):
            for i in range(2):
                tot = gpart[hh, 0, a, i].astype(jnp.float32) + crecv[hh, a, i].astype(jnp.float32)
                fsend[hh, i, :, a] = tot.astype(jnp.bfloat16).reshape(H, TOK // H, HD)
        for n, (dz, dh) in enumerate(final):
            begin(rcopy(
                fsend.at[hh, dz, up(h, dh, H)], frecv.at[hh, dz, h],
                fss.at[hh, n], fsr.at[hh, n], fp[n],
            ))
        frecv[hh, 0, h] = fsend[hh, 0, h]

    c0 = grads(0)
    c1 = grads(1)
    spread(0, c0)
    weight = wrow[...].T
    for cp in dq_x:
        cp.wait_recv()
    for hh in range(HL):
        tot = dqo[:, cols(hh)] * weight[:, hh : hh + 1]
        for e in range(1, X):
            n = e * HL + hh
            tot = tot + rxb[e - 1, :, cols(hh)].astype(jnp.float32) * weight[:, n : n + 1]
        dys[:, :, cols(hh)] = tot.astype(jnp.bfloat16).reshape(Y, SLOTS, HD)
    dq_y = [
        begin(rcopy(dys.at[d], ryb.at[d - 1], dss.at[d - 1], dsr.at[d - 1], yp[Y - d - 1]))
        for d in [Y // 2] + near
    ]
    spread(1, c1)
    c2 = grads(2)
    spread(2, c2)
    for cp in dq_y:
        cp.wait_recv()
    tot = dys[0].astype(jnp.float32)
    for d in range(1, Y):
        tot = tot + ryb[d - 1].astype(jnp.float32)
    dqf[h] = tot.astype(jnp.bfloat16)
    for dh in range(1, H):
        to = dev(z, y, x, c, up(h, dh, H))
        begin(rcopy(dqf.at[h], dqf.at[h], hss.at[dh - 1], hsr.at[dh - 1], to))

    for hh in range(HL):
        for n, (dz, dh) in enumerate(final):
            rcopy(
                fsend.at[hh, 0, 0], frecv.at[hh, dz, dn(h, dh, H)],
                fss.at[hh, n], fsr.at[hh, n], fp[n],
            ).wait_recv()
        for i in range(H):
            lanes = slice(i * FEAT + hh * HD, i * FEAT + (hh + 1) * HD)
            for a in range(2):
                for p in range(2):
                    parts_ref[p, a + 1, :, lanes] = frecv[hh, p, i, a]
    for dh in range(1, H):
        slot = dn(h, dh, H)
        rcopy(dqf.at[slot], dqf.at[slot], hss.at[dh - 1], hsr.at[dh - 1], xp[0]).wait_recv()
    out_rows = TOK // H
    pr = lax.broadcasted_iota(jnp.int32, (out_rows, SLOTS), 0) + h * out_rows
    pj = lax.broadcasted_iota(jnp.int32, (out_rows, SLOTS), 1)
    put = jnp.where(targets(pj) == pr, 1.0, 0.0).astype(jnp.bfloat16)
    for i in range(H):
        lanes = slice(i * FEAT, (i + 1) * FEAT)
        for p in range(2):
            half = jnp.where(pj // (SLOTS // 2) == p, put, jnp.zeros_like(put))
            parts_ref[p, 0, :, lanes] = mm(half, dqf[i], NN).astype(jnp.bfloat16)
    for cp in sent:
        cp.wait_send()


def body(X, Y, H, queries, key_states, value_states, attn_output, grad_output, block_index, valid_count):
    C = Y * SLOTS
    bf, f32 = jnp.bfloat16, jnp.float32
    V = pltpu.VMEM
    D = pltpu.SemaphoreType.DMA
    nf = 2 * H - 1
    scratch = [
        V((TOK, FEAT), bf),
        V((TOK, FEAT), bf),
        V((TOK, FEAT), bf),
        V((X, Y, SLOTS, FEAT), bf),
        V((X, Y, SLOTS, FEAT), bf),
        V((Y, 8, C), f32),
        V((X, 8, C), f32),
        V((4, TOK, FEAT), bf),
        V((4, TOK, FEAT), bf),
        V((HL, HD, KEYS), bf),
        V((X, HL, KEYS, C), f32),
        V((X, HL, KEYS, C), f32),
        V((X, HL, HD, C), f32),
        V((16, C), f32),
        V((16, C), f32),
        V((16, C), f32),
        V((16, C), f32),
        V((16, C), f32),
        V((X - 1, 16, C), f32),
        V((X - 1, 16, C), f32),
        V((Y - 1, 16, C), f32),
        V((X - 1, C, FEAT), bf),
        V((X - 1, C, FEAT), bf),
        V((C, FEAT), f32),
        V((Y, SLOTS, FEAT), bf),
        V((Y - 1, SLOTS, FEAT), bf),
        V((H, SLOTS, FEAT), bf),
        V((HL, 2, 2, 2, TOK, HD), bf),
        V((HL, 2, 2, TOK, HD), bf),
        V((HL, 2, H, 2, TOK // H, HD), bf),
        V((HL, 2, H, 2, TOK // H, HD), bf),
        D((Y - 1,)), D((Y - 1,)),
        D((X - 1,)), D((X - 1,)),
        D((2, Y - 1)), D((2, Y - 1)),
        D((2, Y, X - 1)), D((2, Y, X - 1)),
        D((2, 3)), D((2, 3)),
        D((X - 1,)), D((X - 1,)),
        D((X - 1,)), D((X - 1,)),
        D((Y - 1,)), D((Y - 1,)),
        D((X - 1,)), D((X - 1,)),
        D((Y - 1,)), D((Y - 1,)),
        D((HL,)), D((HL,)),
        D((HL, nf)), D((HL, nf)),
        D((H - 1,)), D((H - 1,)),
        D((5,)),
    ]
    out = jax.ShapeDtypeStruct((TOK // H, H * FEAT), bf)
    parts = jax.ShapeDtypeStruct((2, 3, TOK // H, H * FEAT), bf)
    vm = pl.BlockSpec(memory_space=pltpu.VMEM)
    hb = pl.BlockSpec(memory_space=pltpu.HBM)
    sm = pl.BlockSpec(memory_space=pltpu.SMEM)
    parts = pl.pallas_call(
        functools.partial(kernel, X, Y, H),
        out_shape=parts,
        in_specs=[sm, sm, hb, hb, hb, hb, hb],
        out_specs=vm,
        scratch_shapes=scratch,
        compiler_params=pltpu.CompilerParams(
            collective_id=0, has_side_effects=True, vmem_limit_bytes=63 * 1024 * 1024
        ),
    )(block_index, valid_count, queries, key_states, value_states, attn_output, grad_output)
    return tuple(
        (parts[0, a].astype(f32) + parts[1, a].astype(f32)).astype(bf) for a in range(3)
    )


def build(mesh, X, Y):
    H = mesh.shape["head"]
    in_specs = tuple([P("seq", "head")] * 5) + (P("seq", None), P("seq"))
    out_specs = tuple([P(("seq", "head"), None)] * 3)
    return jax.shard_map(
        functools.partial(body, X, Y, H),
        mesh=mesh, in_specs=in_specs, out_specs=out_specs, check_vma=False,
    )


def solution(mesh):
    return build(mesh, 4, 8)
```

```python
import functools

import jax
import jax.numpy as jnp
from jax import lax
from jax.experimental import pallas as pl
from jax.experimental.pallas import tpu as pltpu
from jax.sharding import PartitionSpec as P

HD = 128
BLK = 4
MB_DEV = 4
HL = 3
FEAT = HL * HD
SLOTS = MB_DEV * BLK
TOK = 128
WIDE = FEAT + HD
KEYS = 4 * TOK
SCALE = HD ** (-0.5)
LOG2E = 1.4426950408889634
MESH = pl.DeviceIdType.MESH
NT = (((1,), (1,)), ((), ()))
NN = (((1,), (0,)), ((), ()))


def mm(a, b, dims):
    return lax.dot_general(a, b, dims, preferred_element_type=jnp.float32)


def cols(hh):
    return slice(hh * HD, (hh + 1) * HD)


def kernel(
    X, Y, H,
    bi_ref, vc_ref, q_hbm, k_ref, v_ref, o_hbm, g_hbm,
    parts_ref,
    q_ref, o_ref, g_ref,
    qbuf, gbuf, kbuf, vbuf, kt, ebuf, dbuf, dqt, mrow, frow, wrow, srow, srow2, sxb, sxl, syb,
    dqs, rxb, dqo, dys, ryb, dqf, gpart, crecv, fsend, frecv,
    ysend, yrecv, xsend, xrecv, kvsend, kvrecv, ssx, srx, slx, rlx, ssy, sry,
    dxs, dxr, dss, dsr, css, csr, fss, fsr, hss, hsr, lsem,
):
    C = Y * SLOTS
    s = lax.axis_index("seq")
    h = lax.axis_index("head")
    c = lax.rem(s, 2)
    x = lax.rem(s // 2, X)
    y = lax.rem(s // (2 * X), Y)
    z = s // (2 * X * Y)

    def dev(z_, y_, x_, c_, h_):
        return {"seq": ((z_ * Y + y_) * X + x_) * 2 + c_, "head": h_}

    def up(v, d, n):
        return lax.rem(v + d, n)

    def dn(v, d, n):
        return lax.rem(v + n - d, n)

    quad = [(0, 1), (1, 0), (1, 1)]
    final = [(dz, dh) for dz in range(2) for dh in range(H) if dz or dh]
    xp = [dev(z, y, up(x, e, X), c, h) for e in range(1, X)]
    yp = [dev(z, up(y, d, Y), x, c, h) for d in range(1, Y)]
    qp = [dev(up(z, dz, 2), y, x, up(c, dc, 2), h) for dz, dc in quad]
    fp = [dev(up(z, dz, 2), y, x, c, up(h, dh, H)) for dz, dh in final]
    extra = [p for p, (dz, dh) in zip(fp, final) if dh]

    barrier = pltpu.get_barrier_semaphore()
    greet = xp + yp + qp + extra
    for p in greet:
        pl.semaphore_signal(barrier, inc=1, device_id=p, device_id_type=MESH)

    local = [
        pltpu.make_async_copy(a, b, lsem.at[i])
        for i, (a, b) in enumerate((
            (q_hbm, q_ref), (g_hbm, g_ref), (o_hbm, o_ref), (k_ref, kbuf.at[0]), (v_ref, vbuf.at[0]),
        ))
    ]
    for cp in local:
        cp.start()

    def rcopy(src, dst, ss, rs, to):
        return pltpu.make_async_remote_copy(
            src_ref=src, dst_ref=dst, send_sem=ss, recv_sem=rs,
            device_id=to, device_id_type=MESH,
        )

    count = vc_ref[0] * BLK
    b = [bi_ref[0, j] * BLK for j in range(MB_DEV)]

    def targets(idx):
        j = idx // BLK
        t = jnp.where(j == 0, b[0], jnp.where(j == 1, b[1], jnp.where(j == 2, b[2], b[3])))
        return jnp.where(idx < count, t + lax.rem(idx, BLK), -1)

    ri = lax.broadcasted_iota(jnp.int32, (SLOTS, TOK), 0)
    li = lax.broadcasted_iota(jnp.int32, (SLOTS, TOK), 1)
    sel = jnp.where(targets(ri) == li, 1.0, 0.0).astype(jnp.bfloat16)
    local[0].wait()
    qbuf[0, 0] = mm(sel, q_ref[...], NN).astype(jnp.bfloat16)
    pl.semaphore_wait(barrier, len(greet))

    near = [t for i in range(1, (Y + 1) // 2) for t in (i, Y - i)]
    xorder = ([2] if X > 2 else []) + [e for e in range(1, X) if e != 2]
    sent = []

    def begin(cp):
        cp.start()
        sent.append(cp)
        return cp

    def ycopy(i, d):
        buf = (qbuf, gbuf)[i]
        return rcopy(buf.at[0, 0], buf.at[0, d], ysend.at[i, d - 1], yrecv.at[i, d - 1], yp[d - 1])

    def xcopy(i, d, e):
        buf = (qbuf, gbuf)[i]
        return rcopy(buf.at[0, d], buf.at[e, d], xsend.at[i, d, e - 1], xrecv.at[i, d, e - 1], xp[e - 1])

    def kvcopy(i, j):
        src, buf = ((k_ref, kbuf), (v_ref, vbuf))[i]
        return rcopy(src, buf.at[j + 1], kvsend.at[i, j], kvrecv.at[i, j], qp[j])

    for d in [Y // 2] + near:
        begin(ycopy(0, d))
    for e in xorder:
        begin(xcopy(0, 0, e))
    for j in (1, 2, 0):
        begin(kvcopy(0, j))
    local[1].wait()
    local[2].wait()
    own_g = mm(sel, g_ref[...], NN)
    prod = own_g * mm(sel, o_ref[...], NN)
    dcol = jnp.zeros((SLOTS, HD), jnp.float32)
    for hh in range(HL):
        dcol = jnp.where(li == hh, jnp.sum(prod[:, cols(hh)], axis=1, keepdims=True), dcol)
    gbuf[0, 0] = jnp.concatenate([own_g.astype(jnp.bfloat16), dcol.astype(jnp.bfloat16)], axis=1)
    for d in [Y // 2] + near:
        begin(ycopy(1, d))
    for j in (1, 2, 0):
        begin(kvcopy(1, j))
    order = near + [Y // 2]
    for d in order:
        ycopy(0, d).wait_recv()
        for e in xorder:
            begin(xcopy(0, d, e))
    for e in xorder:
        for d in [0] + order:
            if d and e == xorder[0]:
                ycopy(1, d).wait_recv()
            begin(xcopy(1, d, e))

    local[3].wait()
    for j in range(3):
        kvcopy(0, j).wait_recv()
    for hh in range(HL):
        kt[hh] = kbuf[:, :, cols(hh)].reshape(KEYS, HD).T

    mrow[...] = jnp.zeros_like(mrow)
    srow[...] = jnp.zeros_like(srow)
    arrive = [e for e in range(1, X) if e != 2] + ([2] if X > 2 else [])

    def score(e):
        for hh in range(HL):
            kh = kbuf[:, :, cols(hh)].reshape(KEYS, HD)
            qh = qbuf[e, :, :, cols(hh)].reshape(C, HD)
            s2 = mm(kh, qh, NT) * (SCALE * LOG2E)
            m = jnp.max(s2, axis=0, keepdims=True)
            ex = jnp.exp2(s2 - m)
            tot = jnp.sum(ex, axis=0, keepdims=True)
            ebuf[e, hh] = ex
            n = e * HL + hh
            mrow[n : n + 1, :] = m
            srow[n : n + 1, :] = m + jnp.log2(tot)

    def combine(parts):
        top = functools.reduce(jnp.maximum, parts)
        return top + jnp.log2(sum(jnp.exp2(p - top) for p in parts))

    score(0)
    for e in arrive:
        for d in [0] + order:
            xcopy(0, d, e).wait_recv()
        score(e)
    stat_y = [
        begin(rcopy(srow, syb.at[d - 1], ssy.at[d - 1], sry.at[d - 1], yp[d - 1]))
        for d in [Y // 2] + near
    ]
    stat_l = [
        begin(rcopy(srow, sxl.at[e - 1], slx.at[e - 1], rlx.at[e - 1], xp[e - 1]))
        for e in range(1, X)
    ]

    def dprobs(e):
        for hh in range(HL):
            vh = vbuf[:, :, cols(hh)].reshape(KEYS, HD)
            lane = lax.broadcasted_iota(jnp.int32, (KEYS, HD), 1)
            neg = jnp.where(lane == hh, -1.0, 0.0).astype(jnp.bfloat16)
            gh = gbuf[e, :, :, cols(hh)].reshape(C, HD)
            dh = gbuf[e, :, :, FEAT:WIDE].reshape(C, HD)
            dp = mm(jnp.concatenate([vh, neg], 1), jnp.concatenate([gh, dh], 1), NT)
            dd = ebuf[e, hh] * dp
            dbuf[e, hh] = dd
            dqt[e, hh] = mm(kt[hh], dd.astype(jnp.bfloat16), NN)

    local[4].wait()
    for j in range(3):
        kvcopy(1, j).wait_recv()

    def scaled(e, hh):
        n = e * HL + hh
        row = jnp.exp2(mrow[n : n + 1, :] - srow[n : n + 1, :])
        return (dqt[e, hh] * (row * SCALE)).T

    dq_x = []
    def send_dq(e):
        for d in [0] + order:
            xcopy(1, d, e).wait_recv()
        dprobs(e)
        for hh in range(HL):
            dqs[e - 1, :, cols(hh)] = scaled(e, hh).astype(jnp.bfloat16)
        dq_x.append(
            begin(rcopy(dqs.at[e - 1], rxb.at[e - 1], dxs.at[e - 1], dxr.at[e - 1], xp[X - e - 1]))
        )
    send_dq(xorder[0])
    dprobs(0)
    for hh in range(HL):
        dqo[:, cols(hh)] = scaled(0, hh)

    for cp in stat_y:
        cp.wait_recv()
    srow2[...] = combine([srow[...]] + [pltpu.roll(syb[d - 1], d * SLOTS, 1) for d in range(1, Y)])
    stat_x = [
        begin(rcopy(srow2, sxb.at[e - 1], ssx.at[e - 1], srx.at[e - 1], xp[e - 1]))
        for e in xorder
    ]
    for e in xorder[1:]:
        send_dq(e)
    for cp in stat_x + stat_l:
        cp.wait_recv()
    for i in range(X):
        rows = slice(i * HL, (i + 1) * HL)
        parts = [srow2[rows, :]]
        for e in range(1, X):
            n = (i - e) % X * HL
            parts.append(sxb[e - 1, n : n + HL, :])
        log_total = combine(parts)
        frow[rows, :] = jnp.exp2(mrow[rows, :] - log_total)
        if i == 0:
            wrow[...] = jnp.zeros_like(wrow)
            wrow[rows, :] = jnp.exp2(srow[rows, :] - log_total)
            for e in range(1, X):
                n = e * HL
                wrow[n : n + HL, :] = jnp.exp2(sxl[X - e - 1, n : n + HL, :] - log_total)

    core = dev(z, y, x, 1 - c, h)

    def grads(hh):
        f = [frow[i * HL + hh : i * HL + hh + 1, :] for i in range(X)]
        w = jnp.concatenate([(ebuf[i, hh] * f[i]).astype(jnp.bfloat16) for i in range(X)], axis=1)
        gvp = mm(w, gbuf[:, :, :, cols(hh)].reshape(X * C, HD), NN)
        ds = jnp.concatenate([(dbuf[i, hh] * f[i]).astype(jnp.bfloat16) for i in range(X)], axis=1)
        gkp = mm(ds, qbuf[:, :, :, cols(hh)].reshape(X * C, HD), NN) * SCALE
        for a, val in enumerate((gkp, gvp)):
            for i in range(4):
                gpart[hh, i % 2, a, i // 2] = val[i * TOK : (i + 1) * TOK].astype(jnp.bfloat16)
        return begin(rcopy(gpart.at[hh, 1], crecv.at[hh], css.at[hh], csr.at[hh], core))

    def spread(hh, cp):
        cp.wait_recv()
        for a in range(2):
            for i in range(2):
                tot = gpart[hh, 0, a, i].astype(jnp.float32) + crecv[hh, a, i].astype(jnp.float32)
                fsend[hh, i, :, a] = tot.astype(jnp.bfloat16).reshape(H, TOK // H, HD)
        for n, (dz, dh) in enumerate(final):
            begin(rcopy(
                fsend.at[hh, dz, up(h, dh, H)], frecv.at[hh, dz, h],
                fss.at[hh, n], fsr.at[hh, n], fp[n],
            ))
        frecv[hh, 0, h] = fsend[hh, 0, h]

    early = len(sent)
    c0 = grads(0)
    c1 = grads(1)
    spread(0, c0)
    weight = wrow[...].T
    for cp in dq_x:
        cp.wait_recv()
    for hh in range(HL):
        tot = dqo[:, cols(hh)] * weight[:, hh : hh + 1]
        for e in range(1, X):
            n = e * HL + hh
            tot = tot + rxb[e - 1, :, cols(hh)].astype(jnp.float32) * weight[:, n : n + 1]
        dys[:, :, cols(hh)] = tot.astype(jnp.bfloat16).reshape(Y, SLOTS, HD)
    dq_y = [
        begin(rcopy(dys.at[d], ryb.at[d - 1], dss.at[d - 1], dsr.at[d - 1], yp[Y - d - 1]))
        for d in [Y // 2] + near
    ]
    spread(1, c1)
    c2 = grads(2)
    spread(2, c2)
    for cp in sent[:early]:
        cp.wait_send()
    for cp in dq_y:
        cp.wait_recv()
    tot = dys[0].astype(jnp.float32)
    for d in range(1, Y):
        tot = tot + ryb[d - 1].astype(jnp.float32)
    dqf[h] = tot.astype(jnp.bfloat16)
    for dh in range(1, H):
        to = dev(z, y, x, c, up(h, dh, H))
        begin(rcopy(dqf.at[h], dqf.at[h], hss.at[dh - 1], hsr.at[dh - 1], to))

    for cp in sent[early:]:
        cp.wait_send()
    for hh in range(HL):
        for n, (dz, dh) in enumerate(final):
            rcopy(
                fsend.at[hh, 0, 0], frecv.at[hh, dz, dn(h, dh, H)],
                fss.at[hh, n], fsr.at[hh, n], fp[n],
            ).wait_recv()
        for i in range(H):
            lanes = slice(i * FEAT + hh * HD, i * FEAT + (hh + 1) * HD)
            for a in range(2):
                for p in range(2):
                    parts_ref[p, a + 1, :, lanes] = frecv[hh, p, i, a]
    for dh in range(1, H):
        slot = dn(h, dh, H)
        rcopy(dqf.at[slot], dqf.at[slot], hss.at[dh - 1], hsr.at[dh - 1], xp[0]).wait_recv()
    out_rows = TOK // H
    pr = lax.broadcasted_iota(jnp.int32, (out_rows, SLOTS), 0) + h * out_rows
    pj = lax.broadcasted_iota(jnp.int32, (out_rows, SLOTS), 1)
    put = jnp.where(targets(pj) == pr, 1.0, 0.0).astype(jnp.bfloat16)
    for i in range(H):
        lanes = slice(i * FEAT, (i + 1) * FEAT)
        for p in range(2):
            half = jnp.where(pj // (SLOTS // 2) == p, put, jnp.zeros_like(put))
            parts_ref[p, 0, :, lanes] = mm(half, dqf[i], NN).astype(jnp.bfloat16)


def body(X, Y, H, queries, key_states, value_states, attn_output, grad_output, block_index, valid_count):
    C = Y * SLOTS
    bf, f32 = jnp.bfloat16, jnp.float32
    V = pltpu.VMEM
    D = pltpu.SemaphoreType.DMA
    nf = 2 * H - 1
    scratch = [
        V((TOK, FEAT), bf),
        V((TOK, FEAT), bf),
        V((TOK, FEAT), bf),
        V((X, Y, SLOTS, FEAT), bf),
        V((X, Y, SLOTS, WIDE), bf),
        V((4, TOK, FEAT), bf),
        V((4, TOK, FEAT), bf),
        V((HL, HD, KEYS), bf),
        V((X, HL, KEYS, C), f32),
        V((X, HL, KEYS, C), f32),
        V((X, HL, HD, C), f32),
        V((16, C), f32),
        V((16, C), f32),
        V((16, C), f32),
        V((16, C), f32),
        V((16, C), f32),
        V((X - 1, 16, C), f32),
        V((X - 1, 16, C), f32),
        V((Y - 1, 16, C), f32),
        V((X - 1, C, FEAT), bf),
        V((X - 1, C, FEAT), bf),
        V((C, FEAT), f32),
        V((Y, SLOTS, FEAT), bf),
        V((Y - 1, SLOTS, FEAT), bf),
        V((H, SLOTS, FEAT), bf),
        V((HL, 2, 2, 2, TOK, HD), bf),
        V((HL, 2, 2, TOK, HD), bf),
        V((HL, 2, H, 2, TOK // H, HD), bf),
        V((HL, 2, H, 2, TOK // H, HD), bf),
        D((2, Y - 1)), D((2, Y - 1)),
        D((2, Y, X - 1)), D((2, Y, X - 1)),
        D((2, 3)), D((2, 3)),
        D((X - 1,)), D((X - 1,)),
        D((X - 1,)), D((X - 1,)),
        D((Y - 1,)), D((Y - 1,)),
        D((X - 1,)), D((X - 1,)),
        D((Y - 1,)), D((Y - 1,)),
        D((HL,)), D((HL,)),
        D((HL, nf)), D((HL, nf)),
        D((H - 1,)), D((H - 1,)),
        D((5,)),
    ]
    out = jax.ShapeDtypeStruct((TOK // H, H * FEAT), bf)
    parts = jax.ShapeDtypeStruct((2, 3, TOK // H, H * FEAT), bf)
    vm = pl.BlockSpec(memory_space=pltpu.VMEM)
    hb = pl.BlockSpec(memory_space=pltpu.HBM)
    sm = pl.BlockSpec(memory_space=pltpu.SMEM)
    parts = pl.pallas_call(
        functools.partial(kernel, X, Y, H),
        out_shape=parts,
        in_specs=[sm, sm, hb, hb, hb, hb, hb],
        out_specs=vm,
        scratch_shapes=scratch,
        compiler_params=pltpu.CompilerParams(
            collective_id=0, has_side_effects=True, vmem_limit_bytes=63 * 1024 * 1024
        ),
    )(block_index, valid_count, queries, key_states, value_states, attn_output, grad_output)
    return tuple(
        (parts[0, a].astype(f32) + parts[1, a].astype(f32)).astype(bf) for a in range(3)
    )


def build(mesh, X, Y):
    H = mesh.shape["head"]
    in_specs = tuple([P("seq", "head")] * 5) + (P("seq", None), P("seq"))
    out_specs = tuple([P(("seq", "head"), None)] * 3)
    return jax.shard_map(
        functools.partial(body, X, Y, H),
        mesh=mesh, in_specs=in_specs, out_specs=out_specs, check_vma=False,
    )


def solution(mesh):
    return build(mesh, 4, 8)
```

```python
import functools

import jax
import jax.numpy as jnp
from jax import lax
from jax.experimental import pallas as pl
from jax.experimental.pallas import tpu as pltpu
from jax.sharding import PartitionSpec as P

HD = 128
BLK = 4
MB_DEV = 4
HL = 3
FEAT = HL * HD
SLOTS = MB_DEV * BLK
TOK = 128
WIDE = FEAT + HD
KEYS = 4 * TOK
SCALE = HD ** (-0.5)
LOG2E = 1.4426950408889634
MESH = pl.DeviceIdType.MESH
NT = (((1,), (1,)), ((), ()))
NN = (((1,), (0,)), ((), ()))


def mm(a, b, dims):
    return lax.dot_general(a, b, dims, preferred_element_type=jnp.float32)


def cols(hh):
    return slice(hh * HD, (hh + 1) * HD)


def kernel(
    X, Y, H,
    bi_ref, vc_ref, q_hbm, k_ref, v_ref, o_hbm, g_hbm,
    parts_ref,
    q_ref, o_ref, g_ref,
    qbuf, gbuf, kbuf, vbuf, kt, ebuf, dbuf, dqt, mrow, frow, wrow, srow, srow2, sxb, sxl, syb,
    dqs, rxb, dqo, dys, ryb, dqf, gpart, crecv, fsend, gqv,
    ysend, yrecv, xsend, xrecv, kvsend, kvrecv, ssx, srx, slx, rlx, ssy, sry,
    dxs, dxr, dss, dsr, css, csr, fss, fsr, hss, hsr, lsem, psem,
):
    C = Y * SLOTS
    s = lax.axis_index("seq")
    h = lax.axis_index("head")
    c = lax.rem(s, 2)
    x = lax.rem(s // 2, X)
    y = lax.rem(s // (2 * X), Y)
    z = s // (2 * X * Y)

    def dev(z_, y_, x_, c_, h_):
        return {"seq": ((z_ * Y + y_) * X + x_) * 2 + c_, "head": h_}

    def up(v, d, n):
        return lax.rem(v + d, n)

    def dn(v, d, n):
        return lax.rem(v + n - d, n)

    quad = [(0, 1), (1, 0), (1, 1)]
    final = [(dz, dh) for dz in range(2) for dh in range(H) if dz or dh]
    xp = [dev(z, y, up(x, e, X), c, h) for e in range(1, X)]
    yp = [dev(z, up(y, d, Y), x, c, h) for d in range(1, Y)]
    qp = [dev(up(z, dz, 2), y, x, up(c, dc, 2), h) for dz, dc in quad]
    fp = [dev(up(z, dz, 2), y, x, c, up(h, dh, H)) for dz, dh in final]
    extra = [p for p, (dz, dh) in zip(fp, final) if dh]

    barrier = pltpu.get_barrier_semaphore()
    greet = xp + yp + qp + extra
    for p in greet:
        pl.semaphore_signal(barrier, inc=1, device_id=p, device_id_type=MESH)

    local = [
        pltpu.make_async_copy(a, b, lsem.at[i])
        for i, (a, b) in enumerate((
            (q_hbm, q_ref), (g_hbm, g_ref), (o_hbm, o_ref), (k_ref, kbuf.at[0]), (v_ref, vbuf.at[0]),
        ))
    ]
    for cp in local:
        cp.start()

    def rcopy(src, dst, ss, rs, to):
        return pltpu.make_async_remote_copy(
            src_ref=src, dst_ref=dst, send_sem=ss, recv_sem=rs,
            device_id=to, device_id_type=MESH,
        )

    count = vc_ref[0] * BLK
    b = [bi_ref[0, j] * BLK for j in range(MB_DEV)]

    def targets(idx):
        j = idx // BLK
        t = jnp.where(j == 0, b[0], jnp.where(j == 1, b[1], jnp.where(j == 2, b[2], b[3])))
        return jnp.where(idx < count, t + lax.rem(idx, BLK), -1)

    ri = lax.broadcasted_iota(jnp.int32, (SLOTS, TOK), 0)
    li = lax.broadcasted_iota(jnp.int32, (SLOTS, TOK), 1)
    sel = jnp.where(targets(ri) == li, 1.0, 0.0).astype(jnp.bfloat16)
    local[0].wait()
    qbuf[0, 0] = mm(sel, q_ref[...], NN).astype(jnp.bfloat16)
    pl.semaphore_wait(barrier, len(greet))

    near = [t for i in range(1, (Y + 1) // 2) for t in (i, Y - i)]
    xorder = ([2] if X > 2 else []) + [e for e in range(1, X) if e != 2]
    sent = []

    def begin(cp):
        cp.start()
        sent.append(cp)
        return cp

    def ycopy(i, d):
        buf = (qbuf, gbuf)[i]
        return rcopy(buf.at[0, 0], buf.at[0, d], ysend.at[i, d - 1], yrecv.at[i, d - 1], yp[d - 1])

    def xcopy(i, d, e):
        buf = (qbuf, gbuf)[i]
        return rcopy(buf.at[0, d], buf.at[e, d], xsend.at[i, d, e - 1], xrecv.at[i, d, e - 1], xp[e - 1])

    def kvcopy(i, j):
        src, buf = ((k_ref, kbuf), (v_ref, vbuf))[i]
        return rcopy(src, buf.at[j + 1], kvsend.at[i, j], kvrecv.at[i, j], qp[j])

    for d in [Y // 2] + near:
        begin(ycopy(0, d))
    for e in xorder:
        begin(xcopy(0, 0, e))
    for j in (1, 2, 0):
        begin(kvcopy(0, j))
    local[1].wait()
    local[2].wait()
    own_g = mm(sel, g_ref[...], NN)
    prod = own_g * mm(sel, o_ref[...], NN)
    dcol = jnp.zeros((SLOTS, HD), jnp.float32)
    for hh in range(HL):
        dcol = jnp.where(li == hh, jnp.sum(prod[:, cols(hh)], axis=1, keepdims=True), dcol)
    gbuf[0, 0] = jnp.concatenate([own_g.astype(jnp.bfloat16), dcol.astype(jnp.bfloat16)], axis=1)
    for d in [Y // 2] + near:
        begin(ycopy(1, d))
    for j in (1, 2, 0):
        begin(kvcopy(1, j))
    order = near + [Y // 2]
    for d in order:
        ycopy(0, d).wait_recv()
        for e in xorder:
            begin(xcopy(0, d, e))
    for e in xorder:
        for d in [0] + order:
            if d and e == xorder[0]:
                ycopy(1, d).wait_recv()
            begin(xcopy(1, d, e))

    local[3].wait()
    for j in range(3):
        kvcopy(0, j).wait_recv()
    for hh in range(HL):
        kt[hh] = kbuf[:, :, cols(hh)].reshape(KEYS, HD).T

    mrow[...] = jnp.zeros_like(mrow)
    srow[...] = jnp.zeros_like(srow)
    arrive = [e for e in range(1, X) if e != 2] + ([2] if X > 2 else [])

    def score(e):
        for hh in range(HL):
            kh = kbuf[:, :, cols(hh)].reshape(KEYS, HD)
            qh = qbuf[e, :, :, cols(hh)].reshape(C, HD)
            s2 = mm(kh, qh, NT) * (SCALE * LOG2E)
            m = jnp.max(s2, axis=0, keepdims=True)
            ex = jnp.exp2(s2 - m)
            tot = jnp.sum(ex, axis=0, keepdims=True)
            ebuf[e, hh] = ex
            n = e * HL + hh
            mrow[n : n + 1, :] = m
            srow[n : n + 1, :] = m + jnp.log2(tot)

    def combine(parts):
        top = functools.reduce(jnp.maximum, parts)
        return top + jnp.log2(sum(jnp.exp2(p - top) for p in parts))

    score(0)
    for e in arrive:
        for d in [0] + order:
            xcopy(0, d, e).wait_recv()
        score(e)
    stat_y = [
        begin(rcopy(srow, syb.at[d - 1], ssy.at[d - 1], sry.at[d - 1], yp[d - 1]))
        for d in [Y // 2] + near
    ]
    stat_l = [
        begin(rcopy(srow, sxl.at[e - 1], slx.at[e - 1], rlx.at[e - 1], xp[e - 1]))
        for e in range(1, X)
    ]

    def dprobs(e):
        for hh in range(HL):
            vh = vbuf[:, :, cols(hh)].reshape(KEYS, HD)
            lane = lax.broadcasted_iota(jnp.int32, (KEYS, HD), 1)
            neg = jnp.where(lane == hh, -1.0, 0.0).astype(jnp.bfloat16)
            gh = gbuf[e, :, :, cols(hh)].reshape(C, HD)
            dh = gbuf[e, :, :, FEAT:WIDE].reshape(C, HD)
            dp = mm(jnp.concatenate([vh, neg], 1), jnp.concatenate([gh, dh], 1), NT)
            dd = ebuf[e, hh] * dp
            dbuf[e, hh] = dd
            dqt[e, hh] = mm(kt[hh], dd.astype(jnp.bfloat16), NN)

    local[4].wait()
    for j in range(3):
        kvcopy(1, j).wait_recv()

    def scaled(e, hh):
        n = e * HL + hh
        row = jnp.exp2(mrow[n : n + 1, :] - srow[n : n + 1, :])
        return (dqt[e, hh] * (row * SCALE)).T

    dq_x = []
    def send_dq(e):
        for d in [0] + order:
            xcopy(1, d, e).wait_recv()
        dprobs(e)
        for hh in range(HL):
            dqs[e - 1, :, cols(hh)] = scaled(e, hh).astype(jnp.bfloat16)
        dq_x.append(
            begin(rcopy(dqs.at[e - 1], rxb.at[e - 1], dxs.at[e - 1], dxr.at[e - 1], xp[X - e - 1]))
        )
    send_dq(xorder[0])
    dprobs(0)
    for hh in range(HL):
        dqo[:, cols(hh)] = scaled(0, hh)

    for cp in stat_y:
        cp.wait_recv()
    srow2[...] = combine([srow[...]] + [pltpu.roll(syb[d - 1], d * SLOTS, 1) for d in range(1, Y)])
    stat_x = [
        begin(rcopy(srow2, sxb.at[e - 1], ssx.at[e - 1], srx.at[e - 1], xp[e - 1]))
        for e in xorder
    ]
    for e in xorder[1:]:
        send_dq(e)
    for cp in stat_x + stat_l:
        cp.wait_recv()
    for i in range(X):
        rows = slice(i * HL, (i + 1) * HL)
        parts = [srow2[rows, :]]
        for e in range(1, X):
            n = (i - e) % X * HL
            parts.append(sxb[e - 1, n : n + HL, :])
        log_total = combine(parts)
        frow[rows, :] = jnp.exp2(mrow[rows, :] - log_total)
        if i == 0:
            wrow[...] = jnp.zeros_like(wrow)
            wrow[rows, :] = jnp.exp2(srow[rows, :] - log_total)
            for e in range(1, X):
                n = e * HL
                wrow[n : n + HL, :] = jnp.exp2(sxl[X - e - 1, n : n + HL, :] - log_total)

    core = dev(z, y, x, 1 - c, h)

    def grads(hh):
        f = [frow[i * HL + hh : i * HL + hh + 1, :] for i in range(X)]
        w = jnp.concatenate([(ebuf[i, hh] * f[i]).astype(jnp.bfloat16) for i in range(X)], axis=1)
        gvp = mm(w, gbuf[:, :, :, cols(hh)].reshape(X * C, HD), NN)
        ds = jnp.concatenate([(dbuf[i, hh] * f[i]).astype(jnp.bfloat16) for i in range(X)], axis=1)
        gkp = mm(ds, qbuf[:, :, :, cols(hh)].reshape(X * C, HD), NN) * SCALE
        for a, val in enumerate((gkp, gvp)):
            for i in range(4):
                gpart[hh, i % 2, a, i // 2] = val[i * TOK : (i + 1) * TOK].astype(jnp.bfloat16)
        return begin(rcopy(gpart.at[hh, 1], crecv.at[hh], css.at[hh], csr.at[hh], core))

    kept = []

    def place(hh, dz, head):
        lanes = pl.ds(pl.multiple_of(head * FEAT + hh * HD, HD), HD)
        return parts_ref.at[dz, pl.ds(1, 2), :, lanes]

    def spread(hh, cp):
        cp.wait_recv()
        for a in range(2):
            for i in range(2):
                tot = gpart[hh, 0, a, i].astype(jnp.float32) + crecv[hh, a, i].astype(jnp.float32)
                fsend[hh, i, :, a] = tot.astype(jnp.bfloat16).reshape(H, TOK // H, HD)
        for n, (dz, dh) in enumerate(final):
            begin(rcopy(
                fsend.at[hh, dz, up(h, dh, H)], place(hh, dz, h),
                fss.at[hh, n], fsr.at[hh, n], fp[n],
            ))
        cp = pltpu.make_async_copy(fsend.at[hh, 0, h], place(hh, 0, h), psem.at[hh])
        cp.start()
        kept.append(cp)

    early = len(sent)
    c0 = grads(0)
    c1 = grads(1)
    spread(0, c0)
    weight = wrow[...].T
    for cp in dq_x:
        cp.wait_recv()
    for hh in range(HL):
        tot = dqo[:, cols(hh)] * weight[:, hh : hh + 1]
        for e in range(1, X):
            n = e * HL + hh
            tot = tot + rxb[e - 1, :, cols(hh)].astype(jnp.float32) * weight[:, n : n + 1]
        dys[:, :, cols(hh)] = tot.astype(jnp.bfloat16).reshape(Y, SLOTS, HD)
    dq_y = [
        begin(rcopy(dys.at[d], ryb.at[d - 1], dss.at[d - 1], dsr.at[d - 1], yp[Y - d - 1]))
        for d in [Y // 2] + near
    ]
    spread(1, c1)
    c2 = grads(2)
    spread(2, c2)
    for cp in sent[:early]:
        cp.wait_send()
    for cp in dq_y:
        cp.wait_recv()
    tot = dys[0].astype(jnp.float32)
    for d in range(1, Y):
        tot = tot + ryb[d - 1].astype(jnp.float32)
    dqf[h] = tot.astype(jnp.bfloat16)
    for dh in range(1, H):
        to = dev(z, y, x, c, up(h, dh, H))
        begin(rcopy(dqf.at[h], dqf.at[h], hss.at[dh - 1], hsr.at[dh - 1], to))

    for dh in range(1, H):
        slot = dn(h, dh, H)
        rcopy(dqf.at[slot], dqf.at[slot], hss.at[dh - 1], hsr.at[dh - 1], xp[0]).wait_recv()
    out_rows = TOK // H
    pr = lax.broadcasted_iota(jnp.int32, (out_rows, SLOTS), 0) + h * out_rows
    pj = lax.broadcasted_iota(jnp.int32, (out_rows, SLOTS), 1)
    put = jnp.where(targets(pj) == pr, 1.0, 0.0).astype(jnp.bfloat16)
    for i in range(H):
        lanes = slice(i * FEAT, (i + 1) * FEAT)
        for p in range(2):
            half = jnp.where(pj // (SLOTS // 2) == p, put, jnp.zeros_like(put))
            gqv[p, :, lanes] = mm(half, dqf[i], NN).astype(jnp.bfloat16)
    for p in range(2):
        cp = pltpu.make_async_copy(gqv.at[p], parts_ref.at[p, 0], psem.at[HL + p])
        cp.start()
        kept.append(cp)
    for cp in sent[early:]:
        cp.wait_send()
    for hh in range(HL):
        for n, (dz, dh) in enumerate(final):
            rcopy(
                fsend.at[hh, 0, 0], place(hh, dz, dn(h, dh, H)),
                fss.at[hh, n], fsr.at[hh, n], fp[n],
            ).wait_recv()
    for cp in kept:
        cp.wait()


def body(X, Y, H, queries, key_states, value_states, attn_output, grad_output, block_index, valid_count):
    C = Y * SLOTS
    bf, f32 = jnp.bfloat16, jnp.float32
    V = pltpu.VMEM
    D = pltpu.SemaphoreType.DMA
    nf = 2 * H - 1
    scratch = [
        V((TOK, FEAT), bf),
        V((TOK, FEAT), bf),
        V((TOK, FEAT), bf),
        V((X, Y, SLOTS, FEAT), bf),
        V((X, Y, SLOTS, WIDE), bf),
        V((4, TOK, FEAT), bf),
        V((4, TOK, FEAT), bf),
        V((HL, HD, KEYS), bf),
        V((X, HL, KEYS, C), f32),
        V((X, HL, KEYS, C), f32),
        V((X, HL, HD, C), f32),
        V((16, C), f32),
        V((16, C), f32),
        V((16, C), f32),
        V((16, C), f32),
        V((16, C), f32),
        V((X - 1, 16, C), f32),
        V((X - 1, 16, C), f32),
        V((Y - 1, 16, C), f32),
        V((X - 1, C, FEAT), bf),
        V((X - 1, C, FEAT), bf),
        V((C, FEAT), f32),
        V((Y, SLOTS, FEAT), bf),
        V((Y - 1, SLOTS, FEAT), bf),
        V((H, SLOTS, FEAT), bf),
        V((HL, 2, 2, 2, TOK, HD), bf),
        V((HL, 2, 2, TOK, HD), bf),
        V((HL, 2, H, 2, TOK // H, HD), bf),
        V((2, TOK // H, H * FEAT), bf),
        D((2, Y - 1)), D((2, Y - 1)),
        D((2, Y, X - 1)), D((2, Y, X - 1)),
        D((2, 3)), D((2, 3)),
        D((X - 1,)), D((X - 1,)),
        D((X - 1,)), D((X - 1,)),
        D((Y - 1,)), D((Y - 1,)),
        D((X - 1,)), D((X - 1,)),
        D((Y - 1,)), D((Y - 1,)),
        D((HL,)), D((HL,)),
        D((HL, nf)), D((HL, nf)),
        D((H - 1,)), D((H - 1,)),
        D((5,)),
        D((HL + 2,)),
    ]
    out = jax.ShapeDtypeStruct((TOK // H, H * FEAT), bf)
    parts = jax.ShapeDtypeStruct((2, 3, TOK // H, H * FEAT), bf)
    vm = pl.BlockSpec(memory_space=pltpu.VMEM)
    hb = pl.BlockSpec(memory_space=pltpu.HBM)
    sm = pl.BlockSpec(memory_space=pltpu.SMEM)
    parts = pl.pallas_call(
        functools.partial(kernel, X, Y, H),
        out_shape=parts,
        in_specs=[sm, sm, hb, hb, hb, hb, hb],
        out_specs=hb,
        scratch_shapes=scratch,
        compiler_params=pltpu.CompilerParams(
            collective_id=0, has_side_effects=True, vmem_limit_bytes=63 * 1024 * 1024
        ),
    )(block_index, valid_count, queries, key_states, value_states, attn_output, grad_output)
    return tuple(
        (parts[0, a].astype(f32) + parts[1, a].astype(f32)).astype(bf) for a in range(3)
    )


def build(mesh, X, Y):
    H = mesh.shape["head"]
    in_specs = tuple([P("seq", "head")] * 5) + (P("seq", None), P("seq"))
    out_specs = tuple([P(("seq", "head"), None)] * 3)
    return jax.shard_map(
        functools.partial(body, X, Y, H),
        mesh=mesh, in_specs=in_specs, out_specs=out_specs, check_vma=False,
    )


def solution(mesh):
    return build(mesh, 4, 8)
```
